256 devices in a mesh: sub: 128 (over x_hi, z, y, core), blk: 2 (over x_lo).
Axes of the slice: x: 4 (x_hi: 2, x_lo: 2; x = x_hi * 2 + x_lo), y: 4, z: 8, core: 2. Of those that a mesh axis runs over, the one named last changes fastest.
Arguments:
- source_terms: bfloat16 [2, 105, 2, 32768], P(None, None, None, ('sub', 'blk')), may hold values from -6 to 6
- inverse_blocks: bfloat16 [2, 105, 105, 32768], P(None, None, None, ('sub', 'blk'))
- face_matrices: bfloat16 [4, 105, 105], replicated, may hold values from -0.625 to 0.625
- trace_matrices: bfloat16 [4, 30, 105], replicated, may hold values from -0.625 to 0.625
- neighbours: int32 [32768, 4], P(('sub', 'blk')), may hold values from 0 to 256
- coupling: bfloat16 [32768, 4, 2], P(('sub', 'blk')), may hold values from -0.8984375 to 0.8984375
- slot_faces: int32 [128, 4, 256], P('sub', None, 'blk'), may hold values from 0 to 511
- robin_params: bfloat16 [2, 128, 4, 256], P(None, 'sub', None, 'blk'), may hold values from 0.19921875 to 0.796875
- matching: int32 [4, 128], P(None, 'sub'), may hold values from 0 to 127, as said below
- counts: int32 [4, 128, 2], P(None, 'sub', 'blk'), may hold values from 0 to 128, as said below
Outputs:
- solution: bfloat16 [2, 105, 2, 32768], P(None, None, None, ('sub', 'blk'))
The draws below stay inside these ranges and needn't reach their ends.
Inputs may be any that keep to these rules, and one draw needn't show every extreme that they name: matching[r, s] is the subdomain paired with s in round r, or s itself when s has none; pairing is mutual and a partner lies at most 2 subdomains away from s. counts[r, s, b] is the same at s's partner in round r, and 0 when s has no partner; slot j of block b of s faces slot j of block b of the partner. slot_faces holds 4 e + f for element e of the slot's block and its face f. neighbours holds an element index within the subdomain; the value 256 means no neighbour across that face.
All inputs are finite; a program needn't handle non-finite values.
Results may differ from the reference program's by a relative error of at most 0.025.
Values may be sent and summed in bfloat16 or wider, within the bound.
A program may use at most 128 MiB of HBM per device.

```python
import math
import jax
import jax.numpy as jnp
from jax import lax

DOF = 105
TDOF = 30
E_DEV = 128
SRC = 2
IFACE = 128
ITERS = 2
ROUNDS = 4
E_SUB = 256
ELEMS = 32768
N_SUB = 128
N_BLK = 2


def pairing(key):
    subdomains = jnp.arange(N_SUB, dtype=jnp.int32)
    rows = jnp.arange(ROUNDS, dtype=jnp.int32)
    seg_lengths = jax.random.randint(jax.random.fold_in(key, 31), (ROUNDS, N_SUB), 2, 5).astype(jnp.int32)
    anchor = jax.random.randint(jax.random.fold_in(key, 32), (ROUNDS,), 0, N_SUB // 4 - 1).astype(jnp.int32)
    order_coin = jax.random.randint(jax.random.fold_in(key, 33), (ROUNDS,), 0, 2).astype(jnp.int32)
    seg_lengths = seg_lengths.at[rows, anchor].set(2 + 2 * order_coin)
    seg_lengths = seg_lengths.at[rows, anchor + 1].set(4 - 2 * order_coin)
    starts = (jnp.cumsum(seg_lengths, axis=1) - seg_lengths).astype(jnp.int32)
    segment = jnp.sum((starts[:, None, :] <= subdomains[None, :, None]).astype(jnp.int32), axis=2).astype(jnp.int32) - 1
    seg_start = jnp.take_along_axis(starts, segment, axis=1)
    seg_len = jnp.take_along_axis(seg_lengths, segment, axis=1)
    position = subdomains[None, :] - seg_start
    one = jnp.ones_like(position)
    partner_pos = jnp.where(seg_len == 2, jnp.bitwise_xor(position, one), jnp.where(seg_len == 4, jnp.bitwise_xor(position, 2 * one), 2 - position))
    partner = (seg_start + partner_pos).astype(jnp.int32)
    valid = (partner < N_SUB) & (partner != subdomains[None, :])
    partner = jnp.where(valid, partner, subdomains[None, :])
    forced = (segment == anchor[:, None]) | (segment == anchor[:, None] + 1)
    low_end = jnp.minimum(partner, subdomains[None, :])
    coin_draws = jax.random.randint(jax.random.fold_in(key, 34), (ROUNDS, N_SUB), 0, 4).astype(jnp.int32)
    keep_pair = (jnp.take_along_axis(coin_draws, low_end, axis=1) > 0) | forced
    return jnp.where(keep_pair, partner, subdomains[None, :]).astype(jnp.int32)


def draw_matching(key, part):
    return pairing(key)


def draw_counts(key, part):
    partner = pairing(key)
    subdomains = jnp.arange(N_SUB, dtype=jnp.int32)
    paired = partner != subdomains[None, :]
    low_end = jnp.minimum(partner, subdomains[None, :])
    load_table = jax.random.randint(jax.random.fold_in(key, 13), (ROUNDS, N_SUB, N_BLK), IFACE // 8, IFACE + 1)
    scores = jax.random.randint(jax.random.fold_in(key, 14), (ROUNDS, N_SUB), 0, 1024) * N_SUB + subdomains[None, :]
    scores = jnp.where(paired & (partner > subdomains[None, :]), scores, -1)
    fullest = jnp.argmax(scores, axis=1)
    which_block = jax.random.randint(jax.random.fold_in(key, 15), (ROUNDS,), 0, N_BLK)
    load_table = load_table.at[jnp.arange(ROUNDS), fullest, which_block].set(IFACE)
    slot_loads = jnp.take_along_axis(load_table, jnp.broadcast_to(low_end[:, :, None], (ROUNDS, N_SUB, N_BLK)), axis=1)
    return jnp.where(paired[:, :, None], slot_loads, 0).astype(jnp.int32)


def draw_inverse_blocks(key, part):
    row_index = lax.broadcasted_iota(jnp.int32, (DOF, DOF, 1), 0)
    col_index = lax.broadcasted_iota(jnp.int32, (DOF, DOF, 1), 1)
    diagonal = (row_index == col_index).astype(jnp.float32)
    scatter_part = 0.06 * jax.random.normal(jax.random.fold_in(key, 21), (2, DOF, DOF, ELEMS), jnp.float32)
    level = jnp.exp(jax.random.uniform(jax.random.fold_in(key, 22), (ELEMS,), jnp.float32, math.log(0.5), math.log(1.5)))
    tilt = jax.random.uniform(jax.random.fold_in(key, 23), (ELEMS,), jnp.float32, -0.5, 0.5)
    real_part = scatter_part[0] + diagonal * level
    imag_part = scatter_part[1] + diagonal * (level * tilt)
    return jnp.stack([real_part, imag_part]).astype(jnp.bfloat16)


def place_ends(array, stream_key, smallest, largest):
    longest = array.shape.index(max(array.shape))
    spots = []
    for shift in (0, 1):
        where = [jax.random.randint(jax.random.fold_in(stream_key, axis), (), 0, length) for axis, length in enumerate(array.shape)]
        where[longest] = (where[longest] + shift) % array.shape[longest]
        spots.append(tuple(where))
    return array.at[spots[0]].set(smallest).at[spots[1]].set(largest)


def level_of(own_key, dims, cuts, low, largest):
    factor_of, own = 1.0, jax.random.fold_in(own_key, 6)
    for dim, shards_of in cuts:
        heights = jnp.exp(jax.random.uniform(jax.random.fold_in(own, dim), (shards_of,), jnp.float32, low / len(cuts), largest / len(cuts)))
        factor_of = factor_of * jnp.repeat(heights, dims[dim] // shards_of).reshape([-1 if axis == dim else 1 for axis in range(len(dims))])
    return factor_of


def bell_draw(own_key, shape, spread, bound, split=(), kind=jnp.bfloat16):
    array = jax.random.normal(own_key, shape, jnp.float32) * spread
    if len(split) > 0:
        array = level_of(own_key, shape, split, -0.22, 0.18) * array
    return jnp.clip(array, min=-bound, max=bound).astype(kind)


def setup_inputs(seed: int = 0) -> dict:
    splits = jax.random.split(jax.random.key(seed), 11)
    source_terms = bell_draw(splits[0], (2, DOF, SRC, ELEMS), 1.0, 6.0, ((3, 256),))
    inverse_blocks = draw_inverse_blocks(jax.random.fold_in(splits[10], 71), 0)
    face_matrices = bell_draw(splits[2], (4, DOF, DOF), DOF ** -0.5, 0.625)
    trace_matrices = bell_draw(splits[3], (4, TDOF, DOF), DOF ** -0.5, 0.625)
    neighbours = place_ends(jax.random.randint(splits[4], (ELEMS, 4), 0, E_SUB + 1), jax.random.fold_in(splits[4], 1), 0, E_SUB).astype(jnp.int32)
    coupling = bell_draw(splits[5], (ELEMS, 4, 2), 0.15, 0.8984375, ((0, 256),))
    slot_faces = place_ends(jax.random.randint(splits[6], (N_SUB, ROUNDS, N_BLK * IFACE), 0, 4 * E_DEV), jax.random.fold_in(splits[6], 1), 0, (4 * E_DEV) - 1).astype(jnp.int32)
    robin_params = jnp.clip(0.19921875 + 0.59765625 * jax.random.uniform(splits[7], (2, N_SUB, ROUNDS, N_BLK * IFACE), jnp.float32) ** level_of(splits[7], (2, N_SUB, ROUNDS, N_BLK * IFACE), ((1, 128), (3, 2)), -0.2, 0.2), 0.19921875, 0.796875).astype(jnp.bfloat16)
    matching = draw_matching(jax.random.fold_in(splits[10], 71), 0)
    counts = draw_counts(jax.random.fold_in(splits[10], 71), 0)
    return {"source_terms": source_terms, "inverse_blocks": inverse_blocks, "face_matrices": face_matrices, "trace_matrices": trace_matrices, "neighbours": neighbours, "coupling": coupling, "slot_faces": slot_faces, "robin_params": robin_params, "matching": matching, "counts": counts}


def complex_times(left_re, left_im, right_re, right_im):
    return left_re * right_re - left_im * right_im, left_re * right_im + left_im * right_re


def slot_layout(slot_faces, counts, sub_index, colour):
    slot_codes = slot_faces[sub_index, colour]
    slot_index = jnp.arange(N_BLK * IFACE, dtype=jnp.int32)
    owner_block = slot_index // IFACE
    element = owner_block * E_DEV + slot_codes // 4
    in_use = (slot_index % IFACE) < counts[colour, sub_index][owner_block]
    return element, slot_codes % 4, in_use


def outgoing_traces(sub_index, former, fields, trace_matrices, slot_faces, robin_params, counts, colour):
    element, face_of, in_use = slot_layout(slot_faces, counts, sub_index, colour)
    own_fields = lax.dynamic_slice_in_dim(fields, sub_index * E_SUB, E_SUB, 3)
    picked = jnp.take(own_fields, element, axis=3).astype(jnp.float32)
    chosen = jnp.take(trace_matrices, face_of, axis=0).astype(jnp.float32)
    face_trace = jnp.einsum("jkd,cdsj->cksj", chosen, picked, precision=lax.Precision.HIGHEST)
    robin_re = robin_params[0, sub_index, colour].astype(jnp.float32)
    robin_im = robin_params[1, sub_index, colour].astype(jnp.float32)
    scaled_re, scaled_im = complex_times(robin_re, robin_im, face_trace[0], face_trace[1])
    earlier = former.astype(jnp.float32)
    return jnp.stack([2.0 * scaled_re - earlier[0], 2.0 * scaled_im - earlier[1]]).astype(jnp.bfloat16)


def sweep_one(sub_index, stored, fields, source_terms, inverse_blocks, face_matrices, trace_matrices, neighbours, coupling, slot_faces, counts):
    start = sub_index * E_SUB
    own_fields = lax.dynamic_slice_in_dim(fields, start, E_SUB, 3)
    padded = jnp.concatenate([own_fields, jnp.zeros((2, DOF, SRC, 1), jnp.bfloat16)], axis=3)
    links_here = lax.dynamic_slice_in_dim(neighbours, start, E_SUB, 0)
    weights = lax.dynamic_slice_in_dim(coupling, start, E_SUB, 0).astype(jnp.float32)
    rhs_sum = lax.dynamic_slice_in_dim(source_terms, start, E_SUB, 3).astype(jnp.float32)
    face_wide = face_matrices.astype(jnp.float32)
    for face_no in range(4):
        nearby = jnp.take(padded, links_here[:, face_no], axis=3).astype(jnp.float32)
        coupled = jnp.einsum("kd,cdse->ckse", face_wide[face_no], nearby, precision=lax.Precision.HIGHEST)
        flux_re, flux_im = complex_times(weights[:, face_no, 0], weights[:, face_no, 1], coupled[0], coupled[1])
        rhs_sum = rhs_sum + jnp.stack([flux_re, flux_im])
    trace_wide = trace_matrices.astype(jnp.float32)
    for colour in range(ROUNDS):
        element, face_of, in_use = slot_layout(slot_faces, counts, sub_index, colour)
        chosen = jnp.take(trace_wide, face_of, axis=0)
        slot_lift = jnp.einsum("jkd,cksj->cdsj", chosen, stored[colour].astype(jnp.float32), precision=lax.Precision.HIGHEST)
        slot_lift = lax.optimization_barrier(slot_lift.astype(jnp.bfloat16)).astype(jnp.float32)
        slot_lift = jnp.where(in_use, slot_lift, jnp.zeros_like(slot_lift))
        summed = jax.ops.segment_sum(jnp.moveaxis(slot_lift, 3, 0), element, num_segments=E_SUB)
        rhs_sum = rhs_sum + jnp.moveaxis(summed, 0, 3)
    right_side = lax.optimization_barrier(rhs_sum.astype(jnp.bfloat16)).astype(jnp.float32)
    blocks = lax.dynamic_slice_in_dim(inverse_blocks, start, E_SUB, 3).astype(jnp.float32)
    blocks_first = jnp.moveaxis(blocks, 3, 1)
    side_first = jnp.moveaxis(right_side, 3, 1)

    def apply_block(matrix, vector):
        return jnp.einsum("eij,ejs->eis", matrix, vector, precision=lax.Precision.HIGHEST)

    real_part = apply_block(blocks_first[0], side_first[0]) - apply_block(blocks_first[1], side_first[1])
    imag_part = apply_block(blocks_first[0], side_first[1]) + apply_block(blocks_first[1], side_first[0])
    return jnp.moveaxis(jnp.stack([real_part, imag_part]), 1, 3).astype(jnp.bfloat16)


def reference(source_terms, inverse_blocks, face_matrices, trace_matrices, neighbours, coupling, slot_faces, robin_params, matching, counts):
    fields = jnp.zeros((2, DOF, SRC, ELEMS), jnp.bfloat16)
    interface = jnp.zeros((N_SUB, ROUNDS, 2, TDOF, SRC, N_BLK * IFACE), jnp.bfloat16)
    subdomains = jnp.arange(N_SUB, dtype=jnp.int32)
    slot_index = jnp.arange(N_BLK * IFACE, dtype=jnp.int32)
    owner_block = slot_index // IFACE
    for repeat in range(ITERS):
        for colour in range(ROUNDS):
            def send_one(bundle):
                return outgoing_traces(bundle[0], bundle[1], fields, trace_matrices, slot_faces, robin_params, counts, colour)

            outgoing = lax.map(send_one, (subdomains, interface[:, colour]))
            arrived = jnp.take(outgoing, matching[colour], axis=0)
            in_use = (slot_index % IFACE)[None, :] < jnp.take(counts[colour], owner_block, axis=1)
            updated = jnp.where(in_use[:, None, None, None, :], arrived, interface[:, colour])
            interface = interface.at[:, colour].set(updated)

            def sweep_item(bundle):
                return sweep_one(bundle[0], bundle[1], fields, source_terms, inverse_blocks, face_matrices, trace_matrices, neighbours, coupling, slot_faces, counts)

            pieces = lax.map(sweep_item, (subdomains, interface))
            fields = jnp.moveaxis(pieces, 0, 3).reshape(2, DOF, SRC, ELEMS)
    return fields
```

```python
import functools

import jax
import jax.numpy as jnp
from jax import lax
from jax.experimental import pallas as pl
from jax.experimental.pallas import tpu as pltpu
from jax.sharding import PartitionSpec as P

BF = jnp.bfloat16
F32 = jnp.float32
I32 = jnp.int32
DOF = 105
TDOF = 30
E_DEV = 128
ITERS = 2
ROUNDS = 4
STEPS = ITERS * ROUNDS
L = 128
JP = 112
SHIFTS = (1, -1, 2, -2)
NT = (((1,), (1,)), ((), ()))


def dot(a, b):
    return jnp.dot(a, b, preferred_element_type=F32)


def dot_nt(a, b):
    return lax.dot_general(a, b, NT, preferred_element_type=F32)


def iota(shape, axis):
    return lax.broadcasted_iota(I32, shape, axis)


def hot(mask):
    return jnp.where(mask, 1.0, 0.0).astype(BF)


def row(ref, *index):
    return ref[index[:-1] + (pl.ds(index[-1], 1), slice(None))]


def kernel(
    n_sub,
    inverse,
    source,
    face_t,
    trace_t,
    trace_n,
    neighbours,
    coupling,
    slots,
    robin,
    matching,
    counts,
    out,
    packed,
    tail,
    wide,
    staged,
    weights,
    eye,
    near,
    pick,
    lift_hot,
    to_trace,
    from_trace,
    robin_re,
    robin_im,
    couple,
    base,
    lifted,
    interface,
    rhs,
    left,
    product,
    field,
    far_field,
    outgoing,
    arriving,
    load_sem,
    field_send,
    field_recv,
    robin_send,
    robin_recv,
):
    sub = lax.axis_index("sub")
    blk = lax.axis_index("blk")
    loads = inverse.reshape(DOF, 2 * DOF, L)
    load_main = pltpu.make_async_copy(loads.at[:, pl.ds(0, 208)], packed, load_sem.at[0])
    load_tail = pltpu.make_async_copy(loads.at[:, pl.ds(208, 2)], tail, load_sem.at[1])
    load_main.start()
    load_tail.start()
    arriving[...] = jnp.zeros_like(arriving)

    barrier = pltpu.get_barrier_semaphore()
    for shift in SHIFTS:

        @pl.when((sub + shift >= 0) & (sub + shift < n_sub))
        def _(shift=shift):
            pl.semaphore_signal(
                barrier,
                inc=1,
                device_id=(sub + shift, blk),
                device_id_type=pl.DeviceIdType.MESH,
            )

    pl.semaphore_signal(
        barrier, inc=1, device_id=(sub, 1 - blk), device_id_type=pl.DeviceIdType.MESH
    )

    square = (L, L)
    rows, lanes = iota(square, 0), iota(square, 1)
    eye[...] = hot(rows == lanes)
    identity = eye[...]
    for f in range(4):
        code = jnp.broadcast_to(row(neighbours, f), square)
        mine = hot(code == rows + blk * E_DEV)
        theirs = hot(code == rows + (1 - blk) * E_DEV)
        near[pl.ds(f * L, L), 0:L] = dot_nt(identity, mine).astype(BF)
        near[pl.ds(f * L, L), L : 2 * L] = dot_nt(identity, theirs).astype(BF)
        for c in range(2):
            value = jnp.broadcast_to(row(coupling, f, c), square)
            couple[f, c] = dot_nt(identity, value)
    sign = jnp.where((lanes // 32) % 2 == 0, -2.0, 2.0)
    for r in range(ROUNDS):
        code = jnp.broadcast_to(row(slots, r), square)
        live = lanes < counts[r, 0]
        for f in range(4):
            mask = code == 4 * rows + f
            pick[r, :, pl.ds(f * L, L)] = dot_nt(identity, hot(mask)).astype(BF)
            lift_hot[r, pl.ds(f * L, L), :] = hot(mask & live)
        robin_re[r] = 2.0 * dot_nt(identity, jnp.broadcast_to(row(robin, 0, r), square))
        robin_im[r] = sign * dot_nt(identity, jnp.broadcast_to(row(robin, 1, r), square))
        lifted[r] = jnp.zeros((E_DEV, 4 * L), F32)
        interface[r] = jnp.zeros(square, BF)
    wide_shape = (L, 4 * L)
    fk, lane = iota(wide_shape, 0), iota(wide_shape, 1)
    tall_shape = (4 * L, L)
    trow, tfk = iota(tall_shape, 0), iota(tall_shape, 1)
    for part in range(4):
        spread = hot((lane // L == fk // 32) & (lane % L == part * 32 + fk % 32))
        to_trace[pl.ds(part * L, L), :] = dot(trace_t[...], spread).astype(BF)
        spread = hot((trow // L == tfk // 32) & (trow % L == part * 32 + tfk % 32))
        from_trace[:, pl.ds(part * L, L)] = dot(spread, trace_n[...]).astype(BF)
    base[...] = source[...].astype(F32)
    left[...] = jnp.zeros_like(left)
    rhs[...] = base[...]

    load_main.wait()
    load_tail.wait()

    def widen(i, carry):
        start = pl.multiple_of(i * 224, 8)
        wide[pl.ds(start, 208), :] = packed[i].astype(F32)
        last = tail[i].astype(F32)
        wide[pl.ds(pl.multiple_of(start + 208, 8), 16), :] = jnp.concatenate(
            [last, jnp.zeros((14, L), F32)], axis=0
        )
        return carry

    lax.fori_loop(0, DOF, widen, 0)

    def blank(i, carry):
        wide[pl.ds(pl.multiple_of(i * 224, 8), 224), :] = jnp.zeros((224, L), F32)
        return carry

    lax.fori_loop(DOF, JP, blank, 0)

    def clear(e, carry):
        weights[e, JP:L, :] = jnp.zeros((L - JP, 2 * L), BF)
        return carry

    lax.fori_loop(0, E_DEV, clear, 0)

    def regroup(group, carry):
        for inner in range(16):
            for c in range(2):
                block = wide[pl.ds(group * 32 + 2 * inner + c, JP, stride=224), :]
                block = jnp.concatenate([block, jnp.zeros((L - JP, L), F32)], axis=0).astype(BF)
                staged[c, pl.ds(inner, E_DEV, stride=16), :] = dot_nt(identity, block)

        def pack(chunk, inner_carry):
            for q in range(8):
                e = chunk * 8 + q
                for c in range(2):
                    tile = staged[c, pl.ds(pl.multiple_of(e * 16, 16), 16), :].astype(BF)
                    weights[e, pl.ds(pl.multiple_of(group * 16, 16), 16), c * L : (c + 1) * L] = tile
            return inner_carry

        lax.fori_loop(0, E_DEV // 8, pack, 0)
        return carry

    lax.fori_loop(0, JP // 16, regroup, 0)

    neighbours_there = jnp.int32(1)
    for shift in SHIFTS:
        there = (sub + shift >= 0) & (sub + shift < n_sub)
        neighbours_there = neighbours_there + there.astype(I32)
    pl.semaphore_wait(barrier, neighbours_there)

    def field_copy(slot):
        return pltpu.make_async_remote_copy(
            src_ref=field.at[slot],
            dst_ref=far_field.at[slot],
            send_sem=field_send.at[slot],
            recv_sem=field_recv.at[slot],
            device_id=(sub, 1 - blk),
            device_id_type=pl.DeviceIdType.MESH,
        )

    def robin_copy(slot, which):
        return pltpu.make_async_remote_copy(
            src_ref=outgoing.at[slot],
            dst_ref=arriving.at[slot, which],
            send_sem=robin_send.at[slot, which],
            recv_sem=robin_recv.at[slot, which],
            device_id=(sub + SHIFTS[which], blk),
            device_id_type=pl.DeviceIdType.MESH,
        )

    def exchange(step):
        slot = lax.rem(step, 2)
        r = lax.rem(step, ROUNDS)
        own = field[slot]
        spread = dot(own, to_trace[...]).astype(BF)
        stacked = jnp.concatenate([spread[:, f * L : (f + 1) * L] for f in range(4)], axis=0)
        traced = dot(pick[r], stacked)
        turned = jnp.where(
            (lanes // 32) % 2 == 0, pltpu.roll(traced, L - 32, 1), pltpu.roll(traced, 32, 1)
        )
        former = interface[r]
        sent = robin_re[r] * traced + robin_im[r] * turned - former.astype(F32)
        outgoing[slot] = sent.astype(BF)
        for which, shift in enumerate(SHIFTS):

            @pl.when((sub + shift >= 0) & (sub + shift < n_sub))
            def _(which=which):
                robin_copy(slot, which).start()

        field_copy(slot).wait_recv()
        both = jnp.concatenate([own, far_field[slot]], axis=0)
        total = [base[:, p * L : (p + 1) * L] for p in range(4)]
        for f in range(4):
            gathered = dot(near[pl.ds(f * L, L), :], both).astype(BF)
            flux = [dot(gathered[:, p * L : (p + 1) * L], face_t[f]) for p in range(4)]
            re, im = couple[f, 0], couple[f, 1]
            for s in range(2):
                total[2 * s] += re * flux[2 * s] - im * flux[2 * s + 1]
                total[2 * s + 1] += re * flux[2 * s + 1] + im * flux[2 * s]
        for p in range(4):
            rhs[:, p * L : (p + 1) * L] = total[p]

        for which, shift in enumerate(SHIFTS):

            @pl.when((sub - shift >= 0) & (sub - shift < n_sub))
            def _(which=which):
                robin_copy(slot, which).wait_recv()

        offset = jnp.broadcast_to(matching[r, 0] - sub, square)
        arrived = jnp.zeros(square, BF).astype(F32)
        for which, shift in enumerate(SHIFTS):
            arrived = jnp.where(offset == -shift, arriving[slot, which].astype(F32), arrived)
        live = rows < counts[r, 0]
        updated = jnp.where(live, arrived, former.astype(F32)).astype(BF)
        interface[r] = updated
        landed = dot(lift_hot[r], updated).astype(BF)
        side = jnp.concatenate([landed[f * L : (f + 1) * L] for f in range(4)], axis=1)
        lifted[r] = dot(side, from_trace[...])
        rhs[...] += lifted[0] + lifted[1] + lifted[2] + lifted[3]

        field_copy(slot).wait_send()
        for which, shift in enumerate(SHIFTS):

            @pl.when((sub + shift >= 0) & (sub + shift < n_sub))
            def _(which=which):
                robin_copy(slot, which).wait_send()

    half = E_DEV // 2

    def advance(step, carry):
        pl.when(step > 0)(lambda: exchange(step))
        following = lax.rem(step + 1, 2)
        for el in range(2):
            for c in range(2):
                for s in range(2):
                    p = 2 * s + c
                    left[el, pl.ds(el * 4 + c * 2 + s, half, stride=8), :] = rhs[
                        el * half : (el + 1) * half, p * L : (p + 1) * L
                    ]

        def solve(chunk, inner):
            for q in range(16):
                pair = chunk * 16 + q
                spot = pl.ds(pl.multiple_of(pair * 8, 8), 8)
                vector = jnp.concatenate([left[0, spot, :], left[1, spot, :]], axis=1).astype(BF)
                matrix = jnp.concatenate([weights[pair], weights[half + pair]], axis=0)
                result = dot(vector, matrix)
                product[0, spot, :] = result[:, 0:L]
                product[1, spot, :] = result[:, L : 2 * L]
            return inner

        lax.fori_loop(0, half // 16, solve, 0)
        for el in range(2):
            for s in range(2):
                at = [pl.ds(el * 4 + c * 2 + s, half, stride=8) for c in range(2)]
                re = product[0, at[0], :] - product[1, at[1], :]
                im = product[1, at[0], :] + product[0, at[1], :]
                field[following, el * half : (el + 1) * half, 2 * s * L : (2 * s + 1) * L] = (
                    re.astype(BF)
                )
                field[following, el * half : (el + 1) * half, (2 * s + 1) * L : (2 * s + 2) * L] = (
                    im.astype(BF)
                )

        @pl.when(step < STEPS - 1)
        def _():
            field_copy(following).start()

        return carry

    lax.fori_loop(0, STEPS, advance, 0)
    final = STEPS % 2
    for s in range(2):
        for c in range(2):
            p = 2 * s + c
            out[2 * c + s] = dot_nt(identity, field[final, :, p * L : (p + 1) * L]).astype(BF)


def shards(
    n_sub,
    source_terms,
    inverse_blocks,
    face_matrices,
    trace_matrices,
    neighbours,
    coupling,
    slot_faces,
    robin_params,
    matching,
    counts,
):
    inverse = jnp.transpose(inverse_blocks, (1, 2, 0, 3))
    source = jnp.pad(
        jnp.transpose(source_terms, (3, 2, 0, 1)), ((0, 0), (0, 0), (0, 0), (0, L - DOF))
    ).reshape(E_DEV, 4 * L)
    grow = L - DOF
    face_t = jnp.pad(jnp.transpose(face_matrices, (0, 2, 1)), ((0, 0), (0, grow), (0, grow)))
    trace_n = jnp.pad(trace_matrices, ((0, 0), (0, 32 - TDOF), (0, grow))).reshape(L, L)
    trace_t = jnp.transpose(trace_n)
    vmem = pl.BlockSpec(memory_space=pltpu.VMEM)
    smem = pl.BlockSpec(memory_space=pltpu.SMEM)
    square = (L, L)
    result = pl.pallas_call(
        functools.partial(kernel, n_sub),
        out_shape=jax.ShapeDtypeStruct((4, L, E_DEV), BF),
        in_specs=[pl.BlockSpec(memory_space=pl.ANY)] + [vmem] * 8 + [smem] * 2,
        out_specs=vmem,
        scratch_shapes=[
            pltpu.VMEM((DOF, 208, L), BF),
            pltpu.VMEM((DOF, 2, L), BF),
            pltpu.VMEM((JP * 224, L), F32),
            pltpu.VMEM((2, 16 * E_DEV, L), F32),
            pltpu.VMEM((E_DEV, L, 2 * L), BF),
            pltpu.VMEM(square, BF),
            pltpu.VMEM((4 * L, 2 * L), BF),
            pltpu.VMEM((ROUNDS, L, 4 * L), BF),
            pltpu.VMEM((ROUNDS, 4 * L, L), BF),
            pltpu.VMEM((4 * L, 4 * L), BF),
            pltpu.VMEM((4 * L, 4 * L), BF),
            pltpu.VMEM((ROUNDS, L, L), F32),
            pltpu.VMEM((ROUNDS, L, L), F32),
            pltpu.VMEM((4, 2, L, L), F32),
            pltpu.VMEM((E_DEV, 4 * L), F32),
            pltpu.VMEM((ROUNDS, E_DEV, 4 * L), F32),
            pltpu.VMEM((ROUNDS, L, L), BF),
            pltpu.VMEM((E_DEV, 4 * L), F32),
            pltpu.VMEM((2, 4 * E_DEV, L), F32),
            pltpu.VMEM((2, 4 * E_DEV, L), F32),
            pltpu.VMEM((2, E_DEV, 4 * L), BF),
            pltpu.VMEM((2, E_DEV, 4 * L), BF),
            pltpu.VMEM((2, L, L), BF),
            pltpu.VMEM((2, 4, L, L), BF),
            pltpu.SemaphoreType.DMA((2,)),
            pltpu.SemaphoreType.DMA((2,)),
            pltpu.SemaphoreType.DMA((2,)),
            pltpu.SemaphoreType.DMA((2, 4)),
            pltpu.SemaphoreType.DMA((2, 4)),
        ],
        compiler_params=pltpu.CompilerParams(
            collective_id=0, has_side_effects=True, vmem_limit_bytes=56 * 2**20
        ),
    )(
        inverse,
        source,
        face_t,
        trace_t,
        trace_n,
        jnp.transpose(neighbours),
        jnp.transpose(coupling, (1, 2, 0)),
        slot_faces[0],
        robin_params[:, 0],
        matching,
        counts[:, :, 0],
    )
    return result.reshape(2, 2, L, E_DEV)[:, :, :DOF].transpose(0, 2, 1, 3)


def solution(mesh):
    in_specs = (
        P(None, None, None, ("sub", "blk")),
        P(None, None, None, ("sub", "blk")),
        P(),
        P(),
        P(("sub", "blk"), None),
        P(("sub", "blk"), None, None),
        P("sub", None, "blk"),
        P(None, "sub", None, "blk"),
        P(None, "sub"),
        P(None, "sub", "blk"),
    )
    out_specs = P(None, None, None, ("sub", "blk"))
    body = functools.partial(shards, mesh.shape["sub"])
    return jax.shard_map(body, mesh=mesh, in_specs=in_specs, out_specs=out_specs, check_vma=False)
```

```python
import functools

import jax
import jax.numpy as jnp
from jax import lax
from jax.experimental import pallas as pl
from jax.experimental.pallas import tpu as pltpu
from jax.sharding import PartitionSpec as P

BF = jnp.bfloat16
F32 = jnp.float32
I32 = jnp.int32
DOF = 105
TDOF = 30
E_DEV = 128
ITERS = 2
ROUNDS = 4
STEPS = ITERS * ROUNDS
L = 128
JP = 112
PITCH = 216
PARTS = 3
SHIFTS = (1, -1, 2, -2)
NT = (((1,), (1,)), ((), ()))


def dot(a, b):
    return jnp.dot(a, b, preferred_element_type=F32)


def dot_nt(a, b):
    return lax.dot_general(a, b, NT, preferred_element_type=F32)


def iota(shape, axis):
    return lax.broadcasted_iota(I32, shape, axis)


def hot(mask):
    return jnp.where(mask, 1.0, 0.0).astype(BF)


def row(ref, *index):
    return ref[index[:-1] + (pl.ds(index[-1], 1), slice(None))]


def kernel(
    n_sub,
    inverse,
    source,
    face,
    trace,
    neighbours_in,
    coupling_in,
    slots_in,
    robin_in,
    matching_in,
    counts_in,
    out,
    packed,
    tail,
    source_rows,
    source_tail,
    source_wide,
    face_rows,
    face_tail,
    trace_rows,
    trace_tail,
    face_t,
    neighbours,
    coupling,
    slots,
    robin,
    matching,
    counts,
    wide,
    staged,
    weights,
    eye,
    near,
    pick,
    lift_hot,
    to_trace,
    from_trace,
    robin_re,
    robin_im,
    couple,
    base,
    lifted,
    interface,
    rhs,
    left,
    product,
    field,
    far_field,
    outgoing,
    arriving,
    trace_n_ref,
    eye_wide,
    load_sem,
    field_send,
    field_recv,
    robin_send,
    robin_recv,
):
    sub = lax.axis_index("sub")
    blk = lax.axis_index("blk")
    trace_flat = trace.reshape(4 * TDOF, DOF)
    source_flat = source.reshape(2, 2 * DOF, L)
    face_flat = face.reshape(4 * DOF, DOF)
    loads = inverse.reshape(DOF, 2 * DOF, L)
    small = [
        (slots_in, slots),
        (robin_in, robin),
        (neighbours_in, neighbours),
        (coupling_in, coupling),
        (matching_in, matching),
        (counts_in, counts),
    ]
    moves = [
        (trace_flat.at[pl.ds(0, 112)], trace_rows.at[pl.ds(0, 112)]),
        (trace.at[pl.ds(28, 2)], trace_tail),
        (source_flat.at[:, pl.ds(0, 208)], source_rows),
        (source_flat.at[:, pl.ds(208, 2)], source_tail),
        (loads.at[:, pl.ds(208, 2)], tail),
    ]
    for part in range(PARTS):
        chunk = pl.ds(part * (DOF // PARTS), DOF // PARTS)
        moves.append((loads.at[chunk, pl.ds(0, 208)], packed.at[chunk]))
    moves.append((face_flat.at[pl.ds(0, 416)], face_rows.at[pl.ds(0, 416)]))
    moves.append((face.at[DOF - 1], face_tail))
    moves += small
    moves = [pltpu.make_async_copy(a, b, load_sem.at[n]) for n, (a, b) in enumerate(moves)]
    for move in moves:
        move.start()
    arriving[...] = jnp.zeros_like(arriving)

    barrier = pltpu.get_barrier_semaphore()
    for shift in SHIFTS:

        @pl.when((sub + shift >= 0) & (sub + shift < n_sub))
        def _(shift=shift):
            pl.semaphore_signal(
                barrier,
                inc=1,
                device_id=(sub + shift, blk),
                device_id_type=pl.DeviceIdType.MESH,
            )

    pl.semaphore_signal(
        barrier, inc=1, device_id=(sub, 1 - blk), device_id_type=pl.DeviceIdType.MESH
    )

    square = (L, L)
    rows, lanes = iota(square, 0), iota(square, 1)
    eye[...] = hot(rows == lanes)
    identity = eye[...]
    eye_wide[...] = hot(iota((2 * L, 2 * L), 0) == iota((2 * L, 2 * L), 1))
    left[...] = jnp.zeros_like(left)
    lifted[...] = jnp.zeros_like(lifted)
    interface[...] = jnp.zeros_like(interface)

    first_small = 7 + PARTS
    for n in range(2):
        moves[first_small + n].wait()
    sign = jnp.where((lanes // 32) % 2 == 0, -2.0, 2.0)
    for r in range(ROUNDS):
        code = jnp.broadcast_to(row(slots, r), square)
        for f in range(4):
            pick[r, :, pl.ds(f * L, L)] = dot_nt(identity, hot(code == 4 * rows + f)).astype(BF)
        robin_re[r] = 2.0 * dot_nt(identity, jnp.broadcast_to(row(robin, 0, r), square))
        robin_im[r] = sign * dot_nt(identity, jnp.broadcast_to(row(robin, 1, r), square))
    moves[0].wait()
    moves[1].wait()
    last = trace_tail[...].astype(F32).reshape(8, DOF)
    trace_rows[112:128, :] = jnp.concatenate([last, jnp.zeros((8, DOF), F32)], axis=0).astype(BF)
    trace_n = dot(trace_rows[...], eye[0:DOF, :]).astype(BF)
    trace_t = dot_nt(identity, trace_n).astype(BF)
    wide_shape = (L, 4 * L)
    kf, lane = iota(wide_shape, 0), iota(wide_shape, 1)
    for part in range(4):
        spread = hot((lane // L == kf % 4) & (lane % L == part * 32 + kf // 4))
        to_trace[pl.ds(part * L, L), :] = dot(trace_t, spread).astype(BF)

    moves[2].wait()
    moves[3].wait()
    for c in range(2):
        source_wide[pl.ds(c * 256, 208), :] = source_rows[c].astype(F32)
        source_wide[pl.ds(c * 256 + 208, 48), :] = jnp.concatenate(
            [source_tail[c].astype(F32), jnp.zeros((46, L), F32)], axis=0
        )
    for s in range(2):
        for c in range(2):
            p = 2 * s + c
            block = source_wide[pl.ds(c * 256 + s, L, stride=2), :].astype(BF)
            base[:, p * L : (p + 1) * L] = dot_nt(identity, block)

    def rest_of_constants():
        for f in range(4):
            code = jnp.broadcast_to(row(neighbours, f), square)
            mine = hot(code == rows + blk * E_DEV)
            theirs = hot(code == rows + (1 - blk) * E_DEV)
            near[pl.ds(f * L, L), 0:L] = dot_nt(identity, mine).astype(BF)
            near[pl.ds(f * L, L), L : 2 * L] = dot_nt(identity, theirs).astype(BF)
            for c in range(2):
                value = jnp.broadcast_to(row(coupling, f, c), square)
                couple[f, c] = dot_nt(identity, value)
        for r in range(ROUNDS):
            code = jnp.broadcast_to(row(slots, r), square)
            live = lanes < counts[0, r]
            for f in range(4):
                lift_hot[r, pl.ds(f * L, L), :] = hot((code == 4 * rows + f) & live)
        trow, tkf = iota((4 * L, L), 0), iota((4 * L, L), 1)
        for part in range(4):
            spread = hot((trow // L == tkf % 4) & (trow % L == part * 32 + tkf // 4))
            from_trace[:, pl.ds(part * L, L)] = dot(spread, trace_n_ref[...]).astype(BF)
        end = jnp.concatenate([face_tail[...].astype(F32), jnp.zeros((12, DOF), F32)], axis=0)
        face_rows[416:432, :] = end.astype(BF)
        frow, fk = iota((L, 432), 0), iota((L, 432), 1)
        for f in range(4):
            chosen = dot(hot(4 * frow + f == fk), face_rows[...]).astype(BF)
            face_t[f] = dot_nt(eye[:, 0:DOF], chosen).astype(BF)

    trace_n_ref[...] = trace_n

    def clear(e, carry):
        for q in range(8):
            weights[e * 8 + q, JP:L, :] = jnp.zeros((L - JP, 2 * L), BF)
        return carry

    lax.fori_loop(0, E_DEV // 8, clear, 0)
    rest = (JP - DOF) * PITCH + 8
    wide[pl.ds(DOF * PITCH, rest), :] = jnp.zeros((rest, L), F32)
    moves[4].wait()

    def widen(chunk, carry):
        for q in range(5):
            i = chunk * 5 + q
            start = pl.multiple_of(i * PITCH, 8)
            wide[pl.ds(start, 208), :] = packed[i].astype(F32)
            wide[pl.ds(pl.multiple_of(start + 208, 8), 8), :] = jnp.concatenate(
                [tail[i].astype(F32), jnp.zeros((6, L), F32)], axis=0
            )
        return carry

    each = DOF // PARTS // 5
    for part in range(PARTS):
        moves[5 + part].wait()
        lax.fori_loop(part * each, (part + 1) * each, widen, 0)
    for n in range(5 + PARTS, 7 + PARTS + len(small)):
        if n not in (first_small, first_small + 1):
            moves[n].wait()

    def regroup(group, carry):
        def block(inner, c):
            value = wide[pl.ds(group * 32 + 2 * inner + c, JP, stride=PITCH), :]
            return jnp.concatenate([value, jnp.zeros((L - JP, L), F32)], axis=0)

        for pair in range(8):
            inners = (2 * pair, 2 * pair + 1)
            if pair in (0, 2, 4, 5, 7):
                both = [
                    jnp.concatenate([block(n, 0), block(n, 1)], axis=0).astype(BF) for n in inners
                ]
                result = dot_nt(eye_wide[...], jnp.concatenate(both, axis=1))
                turned = [
                    [result[n * L : (n + 1) * L, c * L : (c + 1) * L] for c in range(2)]
                    for n in range(2)
                ]
            else:
                turned = [[block(n, c).T for c in range(2)] for n in inners]
            for n, inner in enumerate(inners):
                for c in range(2):
                    staged[c, inner // 8, pl.ds(inner % 8, E_DEV, stride=8), :] = turned[n][c]

        def pack(chunk, inner_carry):
            for q in range(16):
                e = chunk * 16 + q
                spot = pl.ds(pl.multiple_of(e * 8, 8), 8)
                for c in range(2):
                    tile = jnp.concatenate([staged[c, 0, spot, :], staged[c, 1, spot, :]], axis=0)
                    weights[e, pl.ds(pl.multiple_of(group * 16, 16), 16), c * L : (c + 1) * L] = (
                        tile.astype(BF)
                    )
            return inner_carry

        lax.fori_loop(0, E_DEV // 16, pack, 0)
        return carry

    lax.fori_loop(0, JP // 16, regroup, 0)

    neighbours_there = jnp.int32(1)
    for shift in SHIFTS:
        there = (sub + shift >= 0) & (sub + shift < n_sub)
        neighbours_there = neighbours_there + there.astype(I32)
    pl.semaphore_wait(barrier, neighbours_there)

    half = E_DEV // 2

    def field_copy(slot):
        return pltpu.make_async_remote_copy(
            src_ref=field.at[slot],
            dst_ref=far_field.at[slot],
            send_sem=field_send.at[slot],
            recv_sem=field_recv.at[slot],
            device_id=(sub, 1 - blk),
            device_id_type=pl.DeviceIdType.MESH,
        )

    def robin_copy(slot, which):
        return pltpu.make_async_remote_copy(
            src_ref=outgoing.at[slot],
            dst_ref=arriving.at[slot, which],
            send_sem=robin_send.at[slot, which],
            recv_sem=robin_recv.at[slot, which],
            device_id=(sub + SHIFTS[which], blk),
            device_id_type=pl.DeviceIdType.MESH,
        )

    def exchange(step):
        slot = lax.rem(step, 2)
        r = lax.rem(step, ROUNDS)
        own = field[slot]
        spread = dot(own, to_trace[...]).astype(BF)
        stacked = jnp.concatenate([spread[:, f * L : (f + 1) * L] for f in range(4)], axis=0)
        traced = dot(pick[r], stacked)
        turned = jnp.where(
            (lanes // 32) % 2 == 0, pltpu.roll(traced, L - 32, 1), pltpu.roll(traced, 32, 1)
        )
        former = interface[r]
        sent = robin_re[r] * traced + robin_im[r] * turned - former.astype(F32)
        outgoing[slot] = sent.astype(BF)
        for which, shift in enumerate(SHIFTS):

            @pl.when((sub + shift >= 0) & (sub + shift < n_sub))
            def _(which=which):
                robin_copy(slot, which).start()

        pl.when(step == 1)(rest_of_constants)

        field_copy(slot).wait_recv()
        both = jnp.concatenate([own, far_field[slot]], axis=0)
        total = [base[:, p * L : (p + 1) * L] for p in range(4)]
        for f in range(4):
            gathered = dot(near[pl.ds(f * L, L), :], both).astype(BF)
            flux = [dot(gathered[:, p * L : (p + 1) * L], face_t[f]) for p in range(4)]
            re, im = couple[f, 0], couple[f, 1]
            for s in range(2):
                total[2 * s] += re * flux[2 * s] - im * flux[2 * s + 1]
                total[2 * s + 1] += re * flux[2 * s + 1] + im * flux[2 * s]
        for p in range(4):
            at = pl.ds(p * L, L)
            others = [lifted[lax.rem(r + n, ROUNDS), :, at] for n in range(1, ROUNDS)]
            rhs[:, at] = total[p] + (others[0] + others[1] + others[2])

        for which, shift in enumerate(SHIFTS):

            @pl.when((sub - shift >= 0) & (sub - shift < n_sub))
            def _(which=which):
                robin_copy(slot, which).wait_recv()

        offset = jnp.broadcast_to(matching[0, r] - sub, square)
        arrived = jnp.zeros(square, BF).astype(F32)
        for which, shift in enumerate(SHIFTS):
            arrived = jnp.where(offset == -shift, arriving[slot, which].astype(F32), arrived)
        live = rows < counts[0, r]
        updated = jnp.where(live, arrived, former.astype(F32)).astype(BF)
        interface[r] = updated
        landed = dot(lift_hot[r], updated).astype(BF)
        side = jnp.concatenate([landed[f * L : (f + 1) * L] for f in range(4)], axis=1)
        added = dot(side, from_trace[...])
        lifted[r] = added
        lay_out(rhs[...] + added)
        pl.when(step > 1)(lambda: sent_all(1 - slot))

    def sent_all(slot):
        field_copy(slot).wait_send()
        for which, shift in enumerate(SHIFTS):

            @pl.when((sub + shift >= 0) & (sub + shift < n_sub))
            def _(which=which):
                robin_copy(slot, which).wait_send()

    def lay_out(value):
        for el in range(2):
            for c in range(2):
                for s in range(2):
                    p = 2 * s + c
                    left[el, pl.ds(el * 4 + c * 2 + s, half, stride=8), :] = value[
                        el * half : (el + 1) * half, p * L : (p + 1) * L
                    ]

    def advance(step, carry):
        pl.when(step > 0)(lambda: exchange(step))
        following = lax.rem(step + 1, 2)
        for pair in range(half):
            spot = pl.ds(pair * 8, 8)
            vector = jnp.concatenate([left[0, spot, :], left[1, spot, :]], axis=1).astype(BF)
            matrix = jnp.concatenate([weights[pair], weights[half + pair]], axis=0)
            result = dot(vector, matrix)
            product[0, spot, :] = result[:, 0:L]
            product[1, spot, :] = result[:, L : 2 * L]
        for el in range(2):
            for s in range(2):
                at = [pl.ds(el * 4 + c * 2 + s, half, stride=8) for c in range(2)]
                re = product[0, at[0], :] - product[1, at[1], :]
                im = product[1, at[0], :] + product[0, at[1], :]
                field[following, el * half : (el + 1) * half, 2 * s * L : (2 * s + 1) * L] = (
                    re.astype(BF)
                )
                field[following, el * half : (el + 1) * half, (2 * s + 1) * L : (2 * s + 2) * L] = (
                    im.astype(BF)
                )
        @pl.when(step < STEPS - 1)
        def _():
            field_copy(following).start()

        return carry

    lay_out(base[...])
    lax.fori_loop(0, STEPS, advance, 0)
    sent_all((STEPS - 1) % 2)
    final = STEPS % 2
    for s in range(2):
        for c in range(2):
            p = 2 * s + c
            turned = dot_nt(identity, field[final, :, p * L : (p + 1) * L])
            out[2 * c + s] = turned[0:DOF].astype(BF)


def shards(
    n_sub,
    source_terms,
    inverse_blocks,
    face_matrices,
    trace_matrices,
    neighbours,
    coupling,
    slot_faces,
    robin_params,
    matching,
    counts,
):
    square = (L, L)
    result = pl.pallas_call(
        functools.partial(kernel, n_sub),
        out_shape=jax.ShapeDtypeStruct((4, DOF, E_DEV), BF),
        in_specs=[pl.BlockSpec(memory_space=pl.ANY)] * 10,
        out_specs=pl.BlockSpec(memory_space=pltpu.VMEM),
        scratch_shapes=[
            pltpu.VMEM((DOF, 208, L), BF),
            pltpu.VMEM((DOF, 2, L), BF),
            pltpu.VMEM((2, 208, L), BF),
            pltpu.VMEM((2, 2, L), BF),
            pltpu.VMEM((512, L), F32),
            pltpu.VMEM((432, DOF), BF),
            pltpu.VMEM((4, DOF), BF),
            pltpu.VMEM((L, DOF), BF),
            pltpu.VMEM((2, 4, DOF), BF),
            pltpu.VMEM((4, L, L), BF),
            pltpu.VMEM((4, L), I32),
            pltpu.VMEM((4, 2, L), BF),
            pltpu.VMEM((4, L), I32),
            pltpu.VMEM((2, 4, L), BF),
            pltpu.SMEM((1, 4), I32),
            pltpu.SMEM((1, 4), I32),
            pltpu.VMEM((JP * PITCH + 8, L), F32),
            pltpu.VMEM((2, 2, 8 * E_DEV, L), F32),
            pltpu.VMEM((E_DEV, L, 2 * L), BF),
            pltpu.VMEM(square, BF),
            pltpu.VMEM((4 * L, 2 * L), BF),
            pltpu.VMEM((ROUNDS, L, 4 * L), BF),
            pltpu.VMEM((ROUNDS, 4 * L, L), BF),
            pltpu.VMEM((4 * L, 4 * L), BF),
            pltpu.VMEM((4 * L, 4 * L), BF),
            pltpu.VMEM((ROUNDS, L, L), F32),
            pltpu.VMEM((ROUNDS, L, L), F32),
            pltpu.VMEM((4, 2, L, L), F32),
            pltpu.VMEM((E_DEV, 4 * L), F32),
            pltpu.VMEM((ROUNDS, E_DEV, 4 * L), F32),
            pltpu.VMEM((ROUNDS, L, L), BF),
            pltpu.VMEM((E_DEV, 4 * L), F32),
            pltpu.VMEM((2, 4 * E_DEV, L), F32),
            pltpu.VMEM((2, 4 * E_DEV, L), F32),
            pltpu.VMEM((2, E_DEV, 4 * L), BF),
            pltpu.VMEM((2, E_DEV, 4 * L), BF),
            pltpu.VMEM((2, L, L), BF),
            pltpu.VMEM((2, 4, L, L), BF),
            pltpu.VMEM(square, BF),
            pltpu.VMEM((2 * L, 2 * L), BF),
            pltpu.SemaphoreType.DMA((13 + PARTS,)),
            pltpu.SemaphoreType.DMA((2,)),
            pltpu.SemaphoreType.DMA((2,)),
            pltpu.SemaphoreType.DMA((2, 4)),
            pltpu.SemaphoreType.DMA((2, 4)),
        ],
        compiler_params=pltpu.CompilerParams(
            collective_id=0, has_side_effects=True, vmem_limit_bytes=56 * 2**20
        ),
    )(
        jnp.transpose(inverse_blocks, (1, 2, 0, 3)),
        source_terms,
        jnp.transpose(face_matrices, (1, 0, 2)),
        jnp.transpose(trace_matrices, (1, 0, 2)),
        jnp.transpose(neighbours),
        jnp.transpose(coupling, (1, 2, 0)),
        slot_faces[0],
        robin_params[:, 0],
        jnp.transpose(matching),
        jnp.transpose(counts[:, :, 0]),
    )
    return result.reshape(2, 2, DOF, E_DEV).transpose(0, 2, 1, 3)


def solution(mesh):
    in_specs = (
        P(None, None, None, ("sub", "blk")),
        P(None, None, None, ("sub", "blk")),
        P(),
        P(),
        P(("sub", "blk"), None),
        P(("sub", "blk"), None, None),
        P("sub", None, "blk"),
        P(None, "sub", None, "blk"),
        P(None, "sub"),
        P(None, "sub", "blk"),
    )
    out_specs = P(None, None, None, ("sub", "blk"))
    body = functools.partial(shards, mesh.shape["sub"])
    return jax.shard_map(body, mesh=mesh, in_specs=in_specs, out_specs=out_specs, check_vma=False)
```

```python
import functools

import jax
import jax.numpy as jnp
from jax import lax
from jax.experimental import pallas as pl
from jax.experimental.pallas import tpu as pltpu
from jax.sharding import PartitionSpec as P

BF = jnp.bfloat16
F32 = jnp.float32
I32 = jnp.int32
DOF = 105
TDOF = 30
E_DEV = 128
ITERS = 2
ROUNDS = 4
STEPS = ITERS * ROUNDS
L = 128
JP = 112
PITCH = 216
SHIFTS = (1, -1, 2, -2)
NT = (((1,), (1,)), ((), ()))


def dot(a, b):
    return jnp.dot(a, b, preferred_element_type=F32)


def dot_nt(a, b):
    return lax.dot_general(a, b, NT, preferred_element_type=F32)


def iota(shape, axis):
    return lax.broadcasted_iota(I32, shape, axis)


def hot(mask):
    return jnp.where(mask, 1.0, 0.0).astype(BF)


def row(ref, *index):
    return ref[index[:-1] + (pl.ds(index[-1], 1), slice(None))]


def kernel(
    n_sub,
    inverse,
    source,
    face,
    trace,
    neighbours_in,
    coupling_in,
    slots_in,
    robin_in,
    matching_in,
    counts_in,
    out,
    packed,
    tail,
    source_rows,
    source_tail,
    source_wide,
    face_rows,
    face_tail,
    trace_rows,
    trace_tail,
    face_t,
    neighbours,
    coupling,
    slots,
    robin,
    matching,
    counts,
    wide,
    staged,
    weights,
    eye,
    near,
    pick,
    lift_hot,
    to_trace,
    from_trace,
    robin_re,
    robin_im,
    couple,
    base,
    lifted,
    interface,
    rhs,
    left,
    product,
    field,
    far_field,
    outgoing,
    arriving,
    trace_n_ref,
    eye_wide,
    load_sem,
    rows_sem,
    field_send,
    field_recv,
    robin_send,
    robin_recv,
):
    sub = lax.axis_index("sub")
    blk = lax.axis_index("blk")
    trace_flat = trace.reshape(4 * TDOF, DOF)
    source_flat = source.reshape(2, 2 * DOF, L)
    face_flat = face.reshape(4 * DOF, DOF)
    loads = inverse.reshape(DOF, 2 * DOF, L)
    def load_rows(group):
        at = pl.ds(pl.multiple_of(group * 32, 32), 32)
        return pltpu.make_async_copy(loads.at[:, at], packed.at[:, at], rows_sem.at[group])

    moves = [
        (slots_in, slots),
        (robin_in, robin),
        (trace_flat.at[pl.ds(0, 112)], trace_rows.at[pl.ds(0, 112)]),
        (trace.at[pl.ds(28, 2)], trace_tail),
        (source_flat.at[:, pl.ds(0, 208)], source_rows),
        (source_flat.at[:, pl.ds(208, 2)], source_tail),
        (loads.at[:, pl.ds(208, 2)], tail),
        (loads.at[:, pl.ds(192, 16)], packed.at[:, pl.ds(192, 16)]),
        (neighbours_in, neighbours),
        (coupling_in, coupling),
        (matching_in, matching),
        (counts_in, counts),
        (face_flat.at[pl.ds(0, 416)], face_rows.at[pl.ds(0, 416)]),
        (face.at[DOF - 1], face_tail),
    ]
    moves = [pltpu.make_async_copy(a, b, load_sem.at[n]) for n, (a, b) in enumerate(moves)]
    for move in moves[:6]:
        move.start()
    for group in range(6):
        load_rows(group).start()
    for move in moves[6:]:
        move.start()
    arriving[...] = jnp.zeros_like(arriving)

    barrier = pltpu.get_barrier_semaphore()
    for shift in SHIFTS:

        @pl.when((sub + shift >= 0) & (sub + shift < n_sub))
        def _(shift=shift):
            pl.semaphore_signal(
                barrier,
                inc=1,
                device_id=(sub + shift, blk),
                device_id_type=pl.DeviceIdType.MESH,
            )

    pl.semaphore_signal(
        barrier, inc=1, device_id=(sub, 1 - blk), device_id_type=pl.DeviceIdType.MESH
    )

    half = E_DEV // 2
    square = (L, L)
    rows, lanes = iota(square, 0), iota(square, 1)
    eye[...] = hot(rows == lanes)
    identity = eye[...]
    eye_wide[...] = hot(iota((2 * L, 2 * L), 0) == iota((2 * L, 2 * L), 1))
    left[1] = jnp.zeros((4 * E_DEV, L), F32)
    interface[...] = jnp.zeros_like(interface)

    def slot_constants(r):
        code = jnp.broadcast_to(row(slots, r), square)
        for f in range(4):
            pick[r, :, pl.ds(f * L, L)] = dot_nt(identity, hot(code == 4 * rows + f)).astype(BF)
        robin_re[r] = 2.0 * dot_nt(identity, jnp.broadcast_to(row(robin, 0, r), square))
        robin_im[r] = sign * dot_nt(identity, jnp.broadcast_to(row(robin, 1, r), square))

    sign = jnp.where((lanes // 32) % 2 == 0, -2.0, 2.0)
    for move in moves[:4]:
        move.wait()
    slot_constants(1)
    last = trace_tail[...].astype(F32).reshape(8, DOF)
    trace_rows[112:128, :] = jnp.concatenate([last, jnp.zeros((8, DOF), F32)], axis=0).astype(BF)
    trace_n = dot(trace_rows[...], eye[0:DOF, :]).astype(BF)
    trace_t = dot_nt(identity, trace_n).astype(BF)
    wide_shape = (L, 4 * L)
    kf, lane = iota(wide_shape, 0), iota(wide_shape, 1)
    for part in range(4):
        spread = hot((lane // L == kf % 4) & (lane % L == part * 32 + kf // 4))
        to_trace[pl.ds(part * L, L), :] = dot(trace_t, spread).astype(BF)

    moves[4].wait()
    moves[5].wait()
    for c in range(2):
        source_wide[pl.ds(c * 256, 208), :] = source_rows[c].astype(F32)
        source_wide[pl.ds(c * 256 + 208, 48), :] = jnp.concatenate(
            [source_tail[c].astype(F32), jnp.zeros((46, L), F32)], axis=0
        )
    for s in range(2):
        for c in range(2):
            p = 2 * s + c
            block = source_wide[pl.ds(c * 256 + s, L, stride=2), :].astype(BF)
            block = jnp.concatenate([block[0:JP], block[96:JP]], axis=0)
            base[:, p * L : (p + 1) * L] = dot_nt(identity, block)

    def rest_of_constants():
        for move in moves[8:]:
            move.wait()
        lifted[...] = jnp.zeros_like(lifted)
        for r in (0, 2, 3):
            slot_constants(r)
        for f in range(4):
            code = jnp.broadcast_to(row(neighbours, f), square)
            mine = hot(code == rows + blk * E_DEV)
            theirs = hot(code == rows + (1 - blk) * E_DEV)
            near[pl.ds(f * L, L), 0:L] = dot_nt(identity, mine).astype(BF)
            near[pl.ds(f * L, L), L : 2 * L] = dot_nt(identity, theirs).astype(BF)
            for c in range(2):
                value = jnp.broadcast_to(row(coupling, f, c), square)
                couple[f, c] = dot_nt(identity, value)
        for r in range(ROUNDS):
            code = jnp.broadcast_to(row(slots, r), square)
            live = lanes < counts[0, r]
            for f in range(4):
                lift_hot[r, pl.ds(f * L, L), :] = hot((code == 4 * rows + f) & live)
        trow, tkf = iota((4 * L, L), 0), iota((4 * L, L), 1)
        folded = jnp.where(lanes >= JP, lanes - 16, lanes)
        repeated = dot(trace_n_ref[...], hot(rows == folded)).astype(BF)
        for part in range(4):
            spread = hot((trow // L == tkf % 4) & (trow % L == part * 32 + tkf // 4))
            from_trace[:, pl.ds(part * L, L)] = dot(spread, repeated).astype(BF)
        end = jnp.concatenate([face_tail[...].astype(F32), jnp.zeros((12, DOF), F32)], axis=0)
        face_rows[416:432, :] = end.astype(BF)
        frow, fk = iota((L, 432), 0), iota((L, 432), 1)
        frow = jnp.where(frow >= JP, frow - 16, frow)
        for f in range(4):
            chosen = dot(hot(4 * frow + f == fk), face_rows[...]).astype(BF)
            face_t[f] = dot_nt(eye[:, 0:DOF], chosen).astype(BF)

    trace_n_ref[...] = trace_n

    rest = (JP - DOF) * PITCH + 8
    wide[pl.ds(DOF * PITCH, rest), :] = jnp.zeros((rest, L), F32)

    def regroup(group, final):
        def widen(chunk, carry):
            for q in range(15):
                i = chunk * 15 + q
                start = i * PITCH + group * 32
                at = pl.multiple_of(group * 32, 32)
                if final:
                    end = jnp.concatenate([tail[i].astype(F32), jnp.zeros((6, L), F32)], axis=0)
                    wide[pl.ds(pl.multiple_of(start, 8), 16), :] = packed[i, 192:208].astype(F32)
                    wide[pl.ds(pl.multiple_of(start + 16, 8), 8), :] = end
                else:
                    wide[pl.ds(pl.multiple_of(start, 8), 32), :] = packed[i, pl.ds(at, 32)].astype(
                        F32
                    )
            return carry

        if final:
            moves[6].wait()
            moves[7].wait()
        else:
            load_rows(group).wait()
        lax.fori_loop(0, DOF // 15, widen, 0)

        def block(inner, c):
            value = wide[pl.ds(group * 32 + 2 * inner + c, JP, stride=PITCH), :]
            return jnp.concatenate([value, jnp.zeros((L - JP, L), F32)], axis=0)

        for pair in range(8):
            inners = (2 * pair, 2 * pair + 1)
            if pair in (0, 2, 4, 5, 7):
                both = [
                    jnp.concatenate([block(n, 0), block(n, 1)], axis=0).astype(BF) for n in inners
                ]
                result = dot_nt(eye_wide[...], jnp.concatenate(both, axis=1))
                turned = [
                    [result[n * L : (n + 1) * L, c * L : (c + 1) * L] for c in range(2)]
                    for n in range(2)
                ]
            else:
                turned = [[block(n, c).T for c in range(2)] for n in inners]
            for n, inner in enumerate(inners):
                for c in range(2):
                    staged[c, inner // 8, pl.ds(inner % 8, E_DEV, stride=8), :] = turned[n][c]

        for later in range(2):
            place = lax.rem(group + later, JP // 16) if not final else (1 - later) * group
            at = pl.ds(pl.multiple_of(place * 16, 16), 16)

            def pack(chunk, inner_carry, at=at):
                for q in range(16):
                    e = chunk * 16 + q
                    spot = pl.ds(pl.multiple_of(e * 8, 8), 8)
                    for c in range(2):
                        tile = jnp.concatenate(
                            [staged[c, 0, spot, :], staged[c, 1, spot, :]], axis=0
                        )
                        weights[e, at, c * L : (c + 1) * L] = tile.astype(BF)
                return inner_carry

            lax.fori_loop(later * half // 16, (later + 1) * half // 16, pack, 0)

    def regroup_step(group, carry):
        regroup(group, False)
        return carry

    lax.fori_loop(0, JP // 16 - 1, regroup_step, 0)
    regroup(JP // 16 - 1, True)

    neighbours_there = jnp.int32(1)
    for shift in SHIFTS:
        there = (sub + shift >= 0) & (sub + shift < n_sub)
        neighbours_there = neighbours_there + there.astype(I32)
    pl.semaphore_wait(barrier, neighbours_there)

    def field_copy(slot):
        return pltpu.make_async_remote_copy(
            src_ref=field.at[slot],
            dst_ref=far_field.at[slot],
            send_sem=field_send.at[slot],
            recv_sem=field_recv.at[slot],
            device_id=(sub, 1 - blk),
            device_id_type=pl.DeviceIdType.MESH,
        )

    def robin_copy(slot, which):
        return pltpu.make_async_remote_copy(
            src_ref=outgoing.at[slot],
            dst_ref=arriving.at[slot, which],
            send_sem=robin_send.at[slot, which],
            recv_sem=robin_recv.at[slot, which],
            device_id=(sub + SHIFTS[which], blk),
            device_id_type=pl.DeviceIdType.MESH,
        )

    def exchange(step):
        slot = lax.rem(step, 2)
        r = lax.rem(step, ROUNDS)
        own = field[slot]
        spread = dot(own, to_trace[...]).astype(BF)
        stacked = jnp.concatenate([spread[:, f * L : (f + 1) * L] for f in range(4)], axis=0)
        traced = dot(pick[r], stacked)
        turned = jnp.where(
            (lanes // 32) % 2 == 0, pltpu.roll(traced, L - 32, 1), pltpu.roll(traced, 32, 1)
        )
        former = interface[r]
        sent = robin_re[r] * traced + robin_im[r] * turned - former.astype(F32)
        outgoing[slot] = sent.astype(BF)
        for which, shift in enumerate(SHIFTS):

            @pl.when((sub + shift >= 0) & (sub + shift < n_sub))
            def _(which=which):
                robin_copy(slot, which).start()

        pl.when(step == 1)(rest_of_constants)

        field_copy(slot).wait_recv()
        both = jnp.concatenate([own, far_field[slot]], axis=0)
        total = [base[:, p * L : (p + 1) * L] for p in range(4)]
        for f in range(4):
            gathered = dot(near[pl.ds(f * L, L), :], both).astype(BF)
            flux = [dot(gathered[:, p * L : (p + 1) * L], face_t[f]) for p in range(4)]
            re, im = couple[f, 0], couple[f, 1]
            for s in range(2):
                total[2 * s] += re * flux[2 * s] - im * flux[2 * s + 1]
                total[2 * s + 1] += re * flux[2 * s + 1] + im * flux[2 * s]
        for p in range(4):
            at = pl.ds(p * L, L)
            others = [lifted[lax.rem(r + n, ROUNDS), :, at] for n in range(1, ROUNDS)]
            rhs[:, at] = total[p] + (others[0] + others[1] + others[2])

        for which, shift in enumerate(SHIFTS):

            @pl.when((sub - shift >= 0) & (sub - shift < n_sub))
            def _(which=which):
                robin_copy(slot, which).wait_recv()

        offset = jnp.broadcast_to(matching[0, r] - sub, square)
        arrived = jnp.zeros(square, BF).astype(F32)
        for which, shift in enumerate(SHIFTS):
            arrived = jnp.where(offset == -shift, arriving[slot, which].astype(F32), arrived)
        live = rows < counts[0, r]
        updated = jnp.where(live, arrived, former.astype(F32)).astype(BF)
        interface[r] = updated
        landed = dot(lift_hot[r], updated).astype(BF)
        side = jnp.concatenate([landed[f * L : (f + 1) * L] for f in range(4)], axis=1)
        added = dot(side, from_trace[...])
        lifted[r] = added
        lay_out(rhs[...] + added)
        pl.when(step > 1)(lambda: sent_all(1 - slot))

    def sent_all(slot):
        field_copy(slot).wait_send()
        for which, shift in enumerate(SHIFTS):

            @pl.when((sub + shift >= 0) & (sub + shift < n_sub))
            def _(which=which):
                robin_copy(slot, which).wait_send()

    def lay_out(value):
        later = iota((half, L), 1) >= JP
        for c in range(2):
            for s in range(2):
                p = 2 * s + c
                first = value[0:half, p * L : (p + 1) * L]
                second = value[half:E_DEV, p * L : (p + 1) * L]
                left[0, pl.ds(c * 2 + s, half, stride=8), :] = jnp.where(later, 0.0, first)
                left[0, pl.ds(4 + c * 2 + s, half, stride=8), :] = jnp.where(later, second, 0.0)
                left[1, pl.ds(4 + c * 2 + s, half, stride=8), :] = second

    def advance(step, carry):
        pl.when(step > 0)(lambda: exchange(step))
        following = lax.rem(step + 1, 2)
        for pair in range(half):
            spot = pl.ds(pair * 8, 8)
            vector = jnp.concatenate([left[0, spot, :], left[1, spot, 0:96]], axis=1).astype(BF)
            matrix = jnp.concatenate([weights[pair], weights[half + pair]], axis=0)
            result = dot(vector, matrix)
            product[0, spot, :] = result[:, 0:L]
            product[1, spot, :] = result[:, L : 2 * L]
        for el in range(2):
            for s in range(2):
                at = [pl.ds(el * 4 + c * 2 + s, half, stride=8) for c in range(2)]
                re = product[0, at[0], :] - product[1, at[1], :]
                im = product[1, at[0], :] + product[0, at[1], :]
                field[following, el * half : (el + 1) * half, 2 * s * L : (2 * s + 1) * L] = (
                    re.astype(BF)
                )
                field[following, el * half : (el + 1) * half, (2 * s + 1) * L : (2 * s + 2) * L] = (
                    im.astype(BF)
                )
        @pl.when(step < STEPS - 1)
        def _():
            field_copy(following).start()

        return carry

    lay_out(base[...])
    lax.fori_loop(0, STEPS, advance, 0)
    sent_all((STEPS - 1) % 2)
    final = STEPS % 2
    for s in range(2):
        for c in range(2):
            p = 2 * s + c
            turned = dot_nt(identity, field[final, :, p * L : (p + 1) * L])
            out[2 * c + s] = turned[0:DOF].astype(BF)


def shards(
    n_sub,
    source_terms,
    inverse_blocks,
    face_matrices,
    trace_matrices,
    neighbours,
    coupling,
    slot_faces,
    robin_params,
    matching,
    counts,
):
    square = (L, L)
    result = pl.pallas_call(
        functools.partial(kernel, n_sub),
        out_shape=jax.ShapeDtypeStruct((4, DOF, E_DEV), BF),
        in_specs=[pl.BlockSpec(memory_space=pl.ANY)] * 10,
        out_specs=pl.BlockSpec(memory_space=pltpu.VMEM),
        scratch_shapes=[
            pltpu.VMEM((DOF, 208, L), BF),
            pltpu.VMEM((DOF, 2, L), BF),
            pltpu.VMEM((2, 208, L), BF),
            pltpu.VMEM((2, 2, L), BF),
            pltpu.VMEM((512, L), F32),
            pltpu.VMEM((432, DOF), BF),
            pltpu.VMEM((4, DOF), BF),
            pltpu.VMEM((L, DOF), BF),
            pltpu.VMEM((2, 4, DOF), BF),
            pltpu.VMEM((4, L, L), BF),
            pltpu.VMEM((4, L), I32),
            pltpu.VMEM((4, 2, L), BF),
            pltpu.VMEM((4, L), I32),
            pltpu.VMEM((2, 4, L), BF),
            pltpu.SMEM((1, 4), I32),
            pltpu.SMEM((1, 4), I32),
            pltpu.VMEM((JP * PITCH + 8, L), F32),
            pltpu.VMEM((2, 2, 8 * E_DEV, L), F32),
            pltpu.VMEM((E_DEV, JP, 2 * L), BF),
            pltpu.VMEM(square, BF),
            pltpu.VMEM((4 * L, 2 * L), BF),
            pltpu.VMEM((ROUNDS, L, 4 * L), BF),
            pltpu.VMEM((ROUNDS, 4 * L, L), BF),
            pltpu.VMEM((4 * L, 4 * L), BF),
            pltpu.VMEM((4 * L, 4 * L), BF),
            pltpu.VMEM((ROUNDS, L, L), F32),
            pltpu.VMEM((ROUNDS, L, L), F32),
            pltpu.VMEM((4, 2, L, L), F32),
            pltpu.VMEM((E_DEV, 4 * L), F32),
            pltpu.VMEM((ROUNDS, E_DEV, 4 * L), F32),
            pltpu.VMEM((ROUNDS, L, L), BF),
            pltpu.VMEM((E_DEV, 4 * L), F32),
            pltpu.VMEM((2, 4 * E_DEV, L), F32),
            pltpu.VMEM((2, 4 * E_DEV, L), F32),
            pltpu.VMEM((2, E_DEV, 4 * L), BF),
            pltpu.VMEM((2, E_DEV, 4 * L), BF),
            pltpu.VMEM((2, L, L), BF),
            pltpu.VMEM((2, 4, L, L), BF),
            pltpu.VMEM(square, BF),
            pltpu.VMEM((2 * L, 2 * L), BF),
            pltpu.SemaphoreType.DMA((14,)),
            pltpu.SemaphoreType.DMA((6,)),
            pltpu.SemaphoreType.DMA((2,)),
            pltpu.SemaphoreType.DMA((2,)),
            pltpu.SemaphoreType.DMA((2, 4)),
            pltpu.SemaphoreType.DMA((2, 4)),
        ],
        compiler_params=pltpu.CompilerParams(
            collective_id=0, has_side_effects=True, vmem_limit_bytes=56 * 2**20
        ),
    )(
        jnp.transpose(inverse_blocks, (1, 2, 0, 3)),
        source_terms,
        jnp.transpose(face_matrices, (1, 0, 2)),
        jnp.transpose(trace_matrices, (1, 0, 2)),
        jnp.transpose(neighbours),
        jnp.transpose(coupling, (1, 2, 0)),
        slot_faces[0],
        robin_params[:, 0],
        jnp.transpose(matching),
        jnp.transpose(counts[:, :, 0]),
    )
    return result.reshape(2, 2, DOF, E_DEV).transpose(0, 2, 1, 3)


def solution(mesh):
    in_specs = (
        P(None, None, None, ("sub", "blk")),
        P(None, None, None, ("sub", "blk")),
        P(),
        P(),
        P(("sub", "blk"), None),
        P(("sub", "blk"), None, None),
        P("sub", None, "blk"),
        P(None, "sub", None, "blk"),
        P(None, "sub"),
        P(None, "sub", "blk"),
    )
    out_specs = P(None, None, None, ("sub", "blk"))
    body = functools.partial(shards, mesh.shape["sub"])
    return jax.shard_map(body, mesh=mesh, in_specs=in_specs, out_specs=out_specs, check_vma=False)
```

```python
import functools

import jax
import jax.numpy as jnp
from jax import lax
from jax.experimental import pallas as pl
from jax.experimental.pallas import tpu as pltpu
from jax.sharding import PartitionSpec as P

BF = jnp.bfloat16
F32 = jnp.float32
I32 = jnp.int32
DOF = 105
TDOF = 30
E_DEV = 128
ITERS = 2
ROUNDS = 4
STEPS = ITERS * ROUNDS
L = 128
JP = 112
PITCH = 216
SHIFTS = (2, -2, 1, -1)
NT = (((1,), (1,)), ((), ()))


def dot(a, b):
    return jnp.dot(a, b, preferred_element_type=F32)


def dot_nt(a, b):
    return lax.dot_general(a, b, NT, preferred_element_type=F32)


def iota(shape, axis):
    return lax.broadcasted_iota(I32, shape, axis)


def hot(mask):
    return jnp.where(mask, 1.0, 0.0).astype(BF)


def row(ref, *index):
    return ref[index[:-1] + (pl.ds(index[-1], 1), slice(None))]


def kernel(
    n_sub,
    inverse,
    source,
    face,
    trace,
    neighbours_in,
    coupling_in,
    slots_in,
    robin_in,
    matching_in,
    counts_in,
    out,
    packed,
    tail,
    source_rows,
    source_tail,
    source_wide,
    face_rows,
    face_tail,
    trace_rows,
    trace_tail,
    face_t,
    neighbours,
    coupling,
    slots,
    robin,
    matching,
    counts,
    wide,
    staged,
    weights,
    eye,
    near,
    pick,
    lift_hot,
    to_trace,
    from_trace,
    robin_re,
    robin_im,
    couple,
    base,
    lifted,
    interface,
    rhs,
    left,
    product,
    field,
    far_field,
    outgoing,
    arriving,
    trace_n_ref,
    eye_wide,
    load_sem,
    rows_sem,
    field_send,
    field_recv,
    robin_send,
    robin_recv,
):
    sub = lax.axis_index("sub")
    blk = lax.axis_index("blk")
    trace_flat = trace.reshape(4 * TDOF, DOF)
    source_flat = source.reshape(2, 2 * DOF, L)
    face_flat = face.reshape(4 * DOF, DOF)
    loads = inverse.reshape(DOF, 2 * DOF, L)
    def load_rows(group):
        at = pl.ds(pl.multiple_of(group * 32, 32), 32)
        return pltpu.make_async_copy(loads.at[:, at], packed.at[:, at], rows_sem.at[group])

    moves = [
        (slots_in, slots),
        (robin_in, robin),
        (trace_flat.at[pl.ds(0, 112)], trace_rows.at[pl.ds(0, 112)]),
        (trace.at[pl.ds(28, 2)], trace_tail),
        (source_flat.at[:, pl.ds(0, 208)], source_rows),
        (source_flat.at[:, pl.ds(208, 2)], source_tail),
        (loads.at[:, pl.ds(208, 2)], tail),
        (loads.at[:, pl.ds(192, 16)], packed.at[:, pl.ds(192, 16)]),
        (neighbours_in, neighbours),
        (coupling_in, coupling),
        (matching_in, matching),
        (counts_in, counts),
        (face_flat.at[pl.ds(0, 416)], face_rows.at[pl.ds(0, 416)]),
        (face.at[DOF - 1], face_tail),
    ]
    moves = [pltpu.make_async_copy(a, b, load_sem.at[n]) for n, (a, b) in enumerate(moves)]
    for move in moves[:6]:
        move.start()
    for group in range(6):
        load_rows(group).start()
    for move in moves[6:]:
        move.start()
    arriving[...] = jnp.zeros_like(arriving)

    barrier = pltpu.get_barrier_semaphore()
    for shift in SHIFTS:

        @pl.when((sub + shift >= 0) & (sub + shift < n_sub))
        def _(shift=shift):
            pl.semaphore_signal(
                barrier,
                inc=1,
                device_id=(sub + shift, blk),
                device_id_type=pl.DeviceIdType.MESH,
            )

    pl.semaphore_signal(
        barrier, inc=1, device_id=(sub, 1 - blk), device_id_type=pl.DeviceIdType.MESH
    )

    half = E_DEV // 2
    square = (L, L)
    rows, lanes = iota(square, 0), iota(square, 1)
    eye[...] = hot(rows == lanes)
    identity = eye[...]
    eye_wide[...] = hot(iota((2 * L, 2 * L), 0) == iota((2 * L, 2 * L), 1))
    left[1] = jnp.zeros((4 * E_DEV, L), F32)
    interface[...] = jnp.zeros_like(interface)

    def slot_constants(r):
        code = jnp.broadcast_to(row(slots, r), square)
        for f in range(4):
            pick[r, :, pl.ds(f * L, L)] = dot_nt(identity, hot(code == 4 * rows + f)).astype(BF)
        robin_re[r] = 2.0 * dot_nt(identity, jnp.broadcast_to(row(robin, 0, r), square))
        robin_im[r] = sign * dot_nt(identity, jnp.broadcast_to(row(robin, 1, r), square))

    sign = jnp.where((lanes // 32) % 2 == 0, -2.0, 2.0)
    for move in moves[:4]:
        move.wait()
    slot_constants(1)
    last = trace_tail[...].astype(F32).reshape(8, DOF)
    trace_rows[112:128, :] = jnp.concatenate([last, jnp.zeros((8, DOF), F32)], axis=0).astype(BF)
    trace_n = dot(trace_rows[...], eye[0:DOF, :]).astype(BF)
    trace_t = dot_nt(identity, trace_n).astype(BF)
    wide_shape = (L, 4 * L)
    kf, lane = iota(wide_shape, 0), iota(wide_shape, 1)
    for part in range(4):
        spread = hot((lane // L == kf % 4) & (lane % L == part * 32 + kf // 4))
        to_trace[pl.ds(part * L, L), :] = dot(trace_t, spread).astype(BF)

    moves[4].wait()
    moves[5].wait()
    for c in range(2):
        source_wide[pl.ds(c * 256, 208), :] = source_rows[c].astype(F32)
        source_wide[pl.ds(c * 256 + 208, 48), :] = jnp.concatenate(
            [source_tail[c].astype(F32), jnp.zeros((46, L), F32)], axis=0
        )
    for s in range(2):
        for c in range(2):
            p = 2 * s + c
            block = source_wide[pl.ds(c * 256 + s, L, stride=2), :].astype(BF)
            block = jnp.concatenate([block[0:JP], block[96:JP]], axis=0)
            base[:, p * L : (p + 1) * L] = dot_nt(identity, block)

    def rest_of_constants():
        for move in moves[8:]:
            move.wait()
        lifted[...] = jnp.zeros_like(lifted)
        for r in (0, 2, 3):
            slot_constants(r)
        for f in range(4):
            code = jnp.broadcast_to(row(neighbours, f), square)
            mine = hot(code == rows + blk * E_DEV)
            theirs = hot(code == rows + (1 - blk) * E_DEV)
            near[pl.ds(f * L, L), 0:L] = dot_nt(identity, mine).astype(BF)
            near[pl.ds(f * L, L), L : 2 * L] = dot_nt(identity, theirs).astype(BF)
            for c in range(2):
                value = jnp.broadcast_to(row(coupling, f, c), square)
                couple[f, c] = dot_nt(identity, value)
        for r in range(ROUNDS):
            code = jnp.broadcast_to(row(slots, r), square)
            live = lanes < counts[0, r]
            for f in range(4):
                lift_hot[r, pl.ds(f * L, L), :] = hot((code == 4 * rows + f) & live)
        trow, tkf = iota((4 * L, L), 0), iota((4 * L, L), 1)
        folded = jnp.where(lanes >= JP, lanes - 16, lanes)
        repeated = dot(trace_n_ref[...], hot(rows == folded)).astype(BF)
        for part in range(4):
            spread = hot((trow // L == tkf % 4) & (trow % L == part * 32 + tkf // 4))
            from_trace[:, pl.ds(part * L, L)] = dot(spread, repeated).astype(BF)
        end = jnp.concatenate([face_tail[...].astype(F32), jnp.zeros((12, DOF), F32)], axis=0)
        face_rows[416:432, :] = end.astype(BF)
        frow, fk = iota((L, 432), 0), iota((L, 432), 1)
        frow = jnp.where(frow >= JP, frow - 16, frow)
        for f in range(4):
            chosen = dot(hot(4 * frow + f == fk), face_rows[...]).astype(BF)
            face_t[f] = dot_nt(eye[:, 0:DOF], chosen).astype(BF)

    trace_n_ref[...] = trace_n

    rest = (JP - DOF) * PITCH + 8
    wide[pl.ds(DOF * PITCH, rest), :] = jnp.zeros((rest, L), F32)

    def widen(group):
        at = pl.ds(pl.multiple_of(group * 32, 32), 32)
        for i in range(DOF):
            start = pl.multiple_of(i * PITCH + group * 32, 8)
            wide[pl.ds(start, 32), :] = packed[i, at].astype(F32)

    def add_tails():
        moves[6].wait()
        moves[7].wait()

        def add_tail(chunk, carry):
            for q in range(15):
                i = chunk * 15 + q
                end = jnp.concatenate([tail[i].astype(F32), jnp.zeros((14, L), F32)], axis=0)
                packed[i, 208:224] = end.astype(BF)
            return carry

        lax.fori_loop(0, DOF // 15, add_tail, 0)

    def regroup(group, final):
        def block(inner, c):
            value = wide[pl.ds(group * 32 + 2 * inner + c, JP, stride=PITCH), :]
            return jnp.concatenate([value, jnp.zeros((L - JP, L), F32)], axis=0)

        for pair in range(8):
            inners = (2 * pair, 2 * pair + 1)
            if pair in (0, 2, 4, 5, 7):
                both = [
                    jnp.concatenate([block(n, 0), block(n, 1)], axis=0).astype(BF) for n in inners
                ]
                result = dot_nt(eye_wide[...], jnp.concatenate(both, axis=1))
                turned = [
                    [result[n * L : (n + 1) * L, c * L : (c + 1) * L] for c in range(2)]
                    for n in range(2)
                ]
            else:
                turned = [[block(n, c).T for c in range(2)] for n in inners]
            for n, inner in enumerate(inners):
                for c in range(2):
                    staged[c, inner // 8, pl.ds(inner % 8, E_DEV, stride=8), :] = turned[n][c]

        if not final:
            widen(group + 1)
        for later in range(2):
            place = lax.rem(group + later, JP // 16) if not final else (1 - later) * group
            at = pl.ds(pl.multiple_of(place * 16, 16), 16)
            for e in range(later * half, (later + 1) * half):
                spot = pl.ds(e * 8, 8)
                for c in range(2):
                    tile = jnp.concatenate([staged[c, 0, spot, :], staged[c, 1, spot, :]], axis=0)
                    weights[e, at, c * L : (c + 1) * L] = tile.astype(BF)

    def regroup_step(group, carry):
        pl.when(group < 5)(lambda: load_rows(group + 1).wait())
        pl.when(group == 5)(add_tails)
        regroup(group, False)
        return carry

    load_rows(0).wait()
    widen(0)
    lax.fori_loop(0, JP // 16 - 1, regroup_step, 0)
    regroup(JP // 16 - 1, True)

    neighbours_there = jnp.int32(1)
    for shift in SHIFTS:
        there = (sub + shift >= 0) & (sub + shift < n_sub)
        neighbours_there = neighbours_there + there.astype(I32)
    pl.semaphore_wait(barrier, neighbours_there)

    def field_copy(slot):
        return pltpu.make_async_remote_copy(
            src_ref=field.at[slot],
            dst_ref=far_field.at[slot],
            send_sem=field_send.at[slot],
            recv_sem=field_recv.at[slot],
            device_id=(sub, 1 - blk),
            device_id_type=pl.DeviceIdType.MESH,
        )

    def robin_copy(slot, which):
        return pltpu.make_async_remote_copy(
            src_ref=outgoing.at[slot],
            dst_ref=arriving.at[slot, which],
            send_sem=robin_send.at[slot, which],
            recv_sem=robin_recv.at[slot, which],
            device_id=(sub + SHIFTS[which], blk),
            device_id_type=pl.DeviceIdType.MESH,
        )

    def exchange(step):
        slot = lax.rem(step, 2)
        r = lax.rem(step, ROUNDS)
        own = field[slot]
        spread = dot(own, to_trace[...]).astype(BF)
        stacked = jnp.concatenate([spread[:, f * L : (f + 1) * L] for f in range(4)], axis=0)
        traced = dot(pick[r], stacked)
        turned = jnp.where(
            (lanes // 32) % 2 == 0, pltpu.roll(traced, L - 32, 1), pltpu.roll(traced, 32, 1)
        )
        former = interface[r]
        sent = robin_re[r] * traced + robin_im[r] * turned - former.astype(F32)
        outgoing[slot] = sent.astype(BF)
        for which, shift in enumerate(SHIFTS):

            @pl.when((sub + shift >= 0) & (sub + shift < n_sub))
            def _(which=which):
                robin_copy(slot, which).start()

        pl.when(step == 1)(rest_of_constants)
        pl.when(step > 1)(lambda: sent_all(1 - slot))

        field_copy(slot).wait_recv()
        both = jnp.concatenate([own, far_field[slot]], axis=0)
        total = [base[:, p * L : (p + 1) * L] for p in range(4)]
        for f in range(4):
            gathered = dot(near[pl.ds(f * L, L), :], both).astype(BF)
            flux = [dot(gathered[:, p * L : (p + 1) * L], face_t[f]) for p in range(4)]
            re, im = couple[f, 0], couple[f, 1]
            for s in range(2):
                total[2 * s] += re * flux[2 * s] - im * flux[2 * s + 1]
                total[2 * s + 1] += re * flux[2 * s + 1] + im * flux[2 * s]
        for p in range(4):
            at = pl.ds(p * L, L)
            others = [lifted[lax.rem(r + n, ROUNDS), :, at] for n in range(1, ROUNDS)]
            rhs[:, at] = total[p] + (others[0] + others[1] + others[2])

        for which, shift in enumerate(SHIFTS):

            @pl.when((sub - shift >= 0) & (sub - shift < n_sub))
            def _(which=which):
                robin_copy(slot, which).wait_recv()

        offset = jnp.broadcast_to(matching[0, r] - sub, square)
        arrived = jnp.zeros(square, BF).astype(F32)
        for which, shift in enumerate(SHIFTS):
            arrived = jnp.where(offset == -shift, arriving[slot, which].astype(F32), arrived)
        live = rows < counts[0, r]
        updated = jnp.where(live, arrived, former.astype(F32)).astype(BF)
        interface[r] = updated
        landed = dot(lift_hot[r], updated).astype(BF)
        side = jnp.concatenate([landed[f * L : (f + 1) * L] for f in range(4)], axis=1)
        added = dot(side, from_trace[...])
        lifted[r] = added
        lay_out(rhs[...] + added)

    def sent_all(slot):
        field_copy(slot).wait_send()
        for which, shift in enumerate(SHIFTS):

            @pl.when((sub + shift >= 0) & (sub + shift < n_sub))
            def _(which=which):
                robin_copy(slot, which).wait_send()

    def lay_out(value):
        later = iota((half, L), 1) >= JP
        for c in range(2):
            for s in range(2):
                p = 2 * s + c
                first = value[0:half, p * L : (p + 1) * L]
                second = value[half:E_DEV, p * L : (p + 1) * L]
                left[0, pl.ds(c * 2 + s, half, stride=8), :] = jnp.where(later, 0.0, first)
                left[0, pl.ds(4 + c * 2 + s, half, stride=8), :] = jnp.where(later, second, 0.0)
                left[1, pl.ds(4 + c * 2 + s, half, stride=8), :] = second

    def advance(step, carry):
        pl.when(step > 0)(lambda: exchange(step))
        following = lax.rem(step + 1, 2)
        for part in range(4):
            size = half // 4
            for pair in range(part * size, (part + 1) * size):
                spot = pl.ds(pair * 8, 8)
                vector = jnp.concatenate([left[0, spot, :], left[1, spot, 0:96]], axis=1).astype(BF)
                matrix = jnp.concatenate([weights[pair], weights[half + pair]], axis=0)
                result = dot(vector, matrix)
                product[0, spot, :] = result[:, 0:L]
                product[1, spot, :] = result[:, L : 2 * L]
            for el in range(2):
                at = pl.ds(el * half + part * size, size)
                for s in range(2):
                    first = part * size * 8 + el * 4 + s
                    pick_re = pl.ds(first, size, stride=8)
                    pick_im = pl.ds(first + 2, size, stride=8)
                    re = product[0, pick_re, :] - product[1, pick_im, :]
                    im = product[1, pick_re, :] + product[0, pick_im, :]
                    field[following, at, 2 * s * L : (2 * s + 1) * L] = re.astype(BF)
                    field[following, at, (2 * s + 1) * L : (2 * s + 2) * L] = im.astype(BF)

        @pl.when(step < STEPS - 1)
        def _():
            field_copy(following).start()

        return carry

    lay_out(base[...])
    lax.fori_loop(0, STEPS, advance, 0)
    sent_all((STEPS - 1) % 2)
    final = STEPS % 2
    for s in range(2):
        for c in range(2):
            p = 2 * s + c
            turned = dot_nt(identity, field[final, :, p * L : (p + 1) * L])
            out[2 * c + s] = turned[0:DOF].astype(BF)


def shards(
    n_sub,
    source_terms,
    inverse_blocks,
    face_matrices,
    trace_matrices,
    neighbours,
    coupling,
    slot_faces,
    robin_params,
    matching,
    counts,
):
    square = (L, L)
    result = pl.pallas_call(
        functools.partial(kernel, n_sub),
        out_shape=jax.ShapeDtypeStruct((4, DOF, E_DEV), BF),
        in_specs=[pl.BlockSpec(memory_space=pl.ANY)] * 10,
        out_specs=pl.BlockSpec(memory_space=pltpu.VMEM),
        scratch_shapes=[
            pltpu.VMEM((DOF, 224, L), BF),
            pltpu.VMEM((DOF, 2, L), BF),
            pltpu.VMEM((2, 208, L), BF),
            pltpu.VMEM((2, 2, L), BF),
            pltpu.VMEM((512, L), F32),
            pltpu.VMEM((432, DOF), BF),
            pltpu.VMEM((4, DOF), BF),
            pltpu.VMEM((L, DOF), BF),
            pltpu.VMEM((2, 4, DOF), BF),
            pltpu.VMEM((4, L, L), BF),
            pltpu.VMEM((4, L), I32),
            pltpu.VMEM((4, 2, L), BF),
            pltpu.VMEM((4, L), I32),
            pltpu.VMEM((2, 4, L), BF),
            pltpu.SMEM((1, 4), I32),
            pltpu.SMEM((1, 4), I32),
            pltpu.VMEM((JP * PITCH + 8, L), F32),
            pltpu.VMEM((2, 2, 8 * E_DEV, L), F32),
            pltpu.VMEM((E_DEV, JP, 2 * L), BF),
            pltpu.VMEM(square, BF),
            pltpu.VMEM((4 * L, 2 * L), BF),
            pltpu.VMEM((ROUNDS, L, 4 * L), BF),
            pltpu.VMEM((ROUNDS, 4 * L, L), BF),
            pltpu.VMEM((4 * L, 4 * L), BF),
            pltpu.VMEM((4 * L, 4 * L), BF),
            pltpu.VMEM((ROUNDS, L, L), F32),
            pltpu.VMEM((ROUNDS, L, L), F32),
            pltpu.VMEM((4, 2, L, L), F32),
            pltpu.VMEM((E_DEV, 4 * L), F32),
            pltpu.VMEM((ROUNDS, E_DEV, 4 * L), F32),
            pltpu.VMEM((ROUNDS, L, L), BF),
            pltpu.VMEM((E_DEV, 4 * L), F32),
            pltpu.VMEM((2, 4 * E_DEV, L), F32),
            pltpu.VMEM((2, 4 * E_DEV, L), F32),
            pltpu.VMEM((2, E_DEV, 4 * L), BF),
            pltpu.VMEM((2, E_DEV, 4 * L), BF),
            pltpu.VMEM((2, L, L), BF),
            pltpu.VMEM((2, 4, L, L), BF),
            pltpu.VMEM(square, BF),
            pltpu.VMEM((2 * L, 2 * L), BF),
            pltpu.SemaphoreType.DMA((14,)),
            pltpu.SemaphoreType.DMA((6,)),
            pltpu.SemaphoreType.DMA((2,)),
            pltpu.SemaphoreType.DMA((2,)),
            pltpu.SemaphoreType.DMA((2, 4)),
            pltpu.SemaphoreType.DMA((2, 4)),
        ],
        compiler_params=pltpu.CompilerParams(
            collective_id=0, has_side_effects=True, vmem_limit_bytes=56 * 2**20
        ),
    )(
        jnp.transpose(inverse_blocks, (1, 2, 0, 3)),
        source_terms,
        jnp.transpose(face_matrices, (1, 0, 2)),
        jnp.transpose(trace_matrices, (1, 0, 2)),
        jnp.transpose(neighbours),
        jnp.transpose(coupling, (1, 2, 0)),
        slot_faces[0],
        robin_params[:, 0],
        jnp.transpose(matching),
        jnp.transpose(counts[:, :, 0]),
    )
    return result.reshape(2, 2, DOF, E_DEV).transpose(0, 2, 1, 3)


def solution(mesh):
    in_specs = (
        P(None, None, None, ("sub", "blk")),
        P(None, None, None, ("sub", "blk")),
        P(),
        P(),
        P(("sub", "blk"), None),
        P(("sub", "blk"), None, None),
        P("sub", None, "blk"),
        P(None, "sub", None, "blk"),
        P(None, "sub"),
        P(None, "sub", "blk"),
    )
    out_specs = P(None, None, None, ("sub", "blk"))
    body = functools.partial(shards, mesh.shape["sub"])
    return jax.shard_map(body, mesh=mesh, in_specs=in_specs, out_specs=out_specs, check_vma=False)
```

```python
import functools

import jax
import jax.numpy as jnp
from jax import lax
from jax.experimental import pallas as pl
from jax.experimental.pallas import tpu as pltpu
from jax.sharding import PartitionSpec as P

BF = jnp.bfloat16
F32 = jnp.float32
I32 = jnp.int32
DOF = 105
TDOF = 30
E_DEV = 128
ITERS = 2
ROUNDS = 4
STEPS = ITERS * ROUNDS
L = 128
JP = 112
PITCH = 216
SHIFTS = (2, -2, 1, -1)
NT = (((1,), (1,)), ((), ()))


def dot(a, b):
    return jnp.dot(a, b, preferred_element_type=F32)


def dot_nt(a, b):
    return lax.dot_general(a, b, NT, preferred_element_type=F32)


def iota(shape, axis):
    return lax.broadcasted_iota(I32, shape, axis)


def hot(mask):
    return jnp.where(mask, 1.0, 0.0).astype(BF)


def row(ref, *index):
    return ref[index[:-1] + (pl.ds(index[-1], 1), slice(None))]


def kernel(
    n_sub,
    inverse,
    source,
    face,
    trace,
    neighbours_in,
    coupling_in,
    slots_in,
    robin_in,
    matching_in,
    counts_in,
    out,
    packed,
    tail,
    source_rows,
    source_tail,
    source_wide,
    face_rows,
    face_tail,
    trace_rows,
    trace_tail,
    face_t,
    neighbours,
    coupling,
    slots,
    robin,
    matching,
    counts,
    wide,
    staged,
    weights,
    eye,
    near,
    pick,
    lift_hot,
    to_trace,
    from_trace,
    robin_re,
    robin_im,
    couple,
    base,
    lifted,
    interface,
    rhs,
    left,
    product,
    field,
    far_field,
    outgoing,
    arriving,
    trace_n_ref,
    eye_wide,
    load_sem,
    rows_sem,
    field_send,
    field_recv,
    robin_send,
    robin_recv,
):
    sub = lax.axis_index("sub")
    blk = lax.axis_index("blk")
    trace_flat = trace.reshape(4 * TDOF, DOF)
    source_flat = source.reshape(2, 2 * DOF, L)
    face_flat = face.reshape(4 * DOF, DOF)
    loads = inverse.reshape(DOF, 2 * DOF, L)
    def load_rows(group):
        at = pl.ds(pl.multiple_of(group * 32, 32), 32)
        return pltpu.make_async_copy(loads.at[:, at], packed.at[:, at], rows_sem.at[group])

    moves = [
        (slots_in, slots),
        (robin_in, robin),
        (trace_flat.at[pl.ds(0, 112)], trace_rows.at[pl.ds(0, 112)]),
        (trace.at[pl.ds(28, 2)], trace_tail),
        (source_flat.at[:, pl.ds(0, 208)], source_rows),
        (source_flat.at[:, pl.ds(208, 2)], source_tail),
        (loads.at[:, pl.ds(208, 2)], tail),
        (loads.at[:, pl.ds(192, 16)], packed.at[:, pl.ds(192, 16)]),
        (neighbours_in, neighbours),
        (coupling_in, coupling),
        (matching_in, matching),
        (counts_in, counts),
        (face_flat.at[pl.ds(0, 416)], face_rows.at[pl.ds(0, 416)]),
        (face.at[DOF - 1], face_tail),
    ]
    moves = [pltpu.make_async_copy(a, b, load_sem.at[n]) for n, (a, b) in enumerate(moves)]
    for move in moves[:6]:
        move.start()
    for group in range(6):
        load_rows(group).start()
    for move in moves[6:]:
        move.start()
    arriving[...] = jnp.zeros_like(arriving)

    barrier = pltpu.get_barrier_semaphore()
    for shift in SHIFTS:

        @pl.when((sub + shift >= 0) & (sub + shift < n_sub))
        def _(shift=shift):
            pl.semaphore_signal(
                barrier,
                inc=1,
                device_id=(sub + shift, blk),
                device_id_type=pl.DeviceIdType.MESH,
            )

    pl.semaphore_signal(
        barrier, inc=1, device_id=(sub, 1 - blk), device_id_type=pl.DeviceIdType.MESH
    )

    half = E_DEV // 2
    square = (L, L)
    rows, lanes = iota(square, 0), iota(square, 1)
    eye[...] = hot(rows == lanes)
    identity = eye[...]
    eye_wide[...] = hot(iota((2 * L, 2 * L), 0) == iota((2 * L, 2 * L), 1))
    left[1] = jnp.zeros((4 * E_DEV, L), F32)
    interface[...] = jnp.zeros_like(interface)

    def slot_constants(r):
        code = jnp.broadcast_to(row(slots, r), square)
        for f in range(4):
            pick[r, :, pl.ds(f * L, L)] = dot_nt(identity, hot(code == 4 * rows + f)).astype(BF)
        robin_re[r] = 2.0 * dot_nt(identity, jnp.broadcast_to(row(robin, 0, r), square))
        robin_im[r] = sign * dot_nt(identity, jnp.broadcast_to(row(robin, 1, r), square))

    sign = jnp.where((lanes // 32) % 2 == 0, -2.0, 2.0)
    for move in moves[:4]:
        move.wait()
    slot_constants(1)
    last = trace_tail[...].astype(F32).reshape(8, DOF)
    trace_rows[112:128, :] = jnp.concatenate([last, jnp.zeros((8, DOF), F32)], axis=0).astype(BF)
    trace_n = dot(trace_rows[...], eye[0:DOF, :]).astype(BF)
    trace_t = dot_nt(identity, trace_n).astype(BF)
    wide_shape = (L, 4 * L)
    kf, lane = iota(wide_shape, 0), iota(wide_shape, 1)
    for part in range(4):
        spread = hot((lane // L == kf % 4) & (lane % L == part * 32 + kf // 4))
        to_trace[pl.ds(part * L, L), :] = dot(trace_t, spread).astype(BF)

    moves[4].wait()
    moves[5].wait()
    for c in range(2):
        source_wide[pl.ds(c * 256, 208), :] = source_rows[c].astype(F32)
        source_wide[pl.ds(c * 256 + 208, 48), :] = jnp.concatenate(
            [source_tail[c].astype(F32), jnp.zeros((46, L), F32)], axis=0
        )
    for s in range(2):
        for c in range(2):
            p = 2 * s + c
            block = source_wide[pl.ds(c * 256 + s, L, stride=2), :].astype(BF)
            block = jnp.concatenate([block[0:JP], block[96:JP]], axis=0)
            base[:, p * L : (p + 1) * L] = dot_nt(identity, block)

    def rest_of_constants():
        for move in moves[8:]:
            move.wait()
        lifted[...] = jnp.zeros_like(lifted)
        for r in (0, 2, 3):
            slot_constants(r)
        for f in range(4):
            code = jnp.broadcast_to(row(neighbours, f), square)
            mine = hot(code == rows + blk * E_DEV)
            theirs = hot(code == rows + (1 - blk) * E_DEV)
            near[pl.ds(f * L, L), 0:L] = dot_nt(identity, mine).astype(BF)
            near[pl.ds(f * L, L), L : 2 * L] = dot_nt(identity, theirs).astype(BF)
            for c in range(2):
                value = jnp.broadcast_to(row(coupling, f, c), square)
                couple[f, c] = dot_nt(identity, value)
        for r in range(ROUNDS):
            code = jnp.broadcast_to(row(slots, r), square)
            live = lanes < counts[0, r]
            for f in range(4):
                lift_hot[r, pl.ds(f * L, L), :] = hot((code == 4 * rows + f) & live)
        trow, tkf = iota((4 * L, L), 0), iota((4 * L, L), 1)
        folded = jnp.where(lanes >= JP, lanes - 16, lanes)
        repeated = dot(trace_n_ref[...], hot(rows == folded)).astype(BF)
        for part in range(4):
            spread = hot((trow // L == tkf % 4) & (trow % L == part * 32 + tkf // 4))
            from_trace[:, pl.ds(part * L, L)] = dot(spread, repeated).astype(BF)
        end = jnp.concatenate([face_tail[...].astype(F32), jnp.zeros((12, DOF), F32)], axis=0)
        face_rows[416:432, :] = end.astype(BF)
        frow, fk = iota((L, 432), 0), iota((L, 432), 1)
        frow = jnp.where(frow >= JP, frow - 16, frow)
        for f in range(4):
            chosen = dot(hot(4 * frow + f == fk), face_rows[...]).astype(BF)
            face_t[f] = dot_nt(eye[:, 0:DOF], chosen).astype(BF)

    trace_n_ref[...] = trace_n

    rest = (JP - DOF) * PITCH + 8
    wide[pl.ds(DOF * PITCH, rest), :] = jnp.zeros((rest, L), F32)

    def widen(group):
        at = pl.ds(pl.multiple_of(group * 32, 32), 32)
        for i in range(DOF):
            start = pl.multiple_of(i * PITCH + group * 32, 8)
            wide[pl.ds(start, 32), :] = packed[i, at].astype(F32)

    def add_tails():
        moves[6].wait()
        moves[7].wait()

        def add_tail(chunk, carry):
            for q in range(15):
                i = chunk * 15 + q
                end = jnp.concatenate([tail[i].astype(F32), jnp.zeros((14, L), F32)], axis=0)
                packed[i, 208:224] = end.astype(BF)
            return carry

        lax.fori_loop(0, DOF // 15, add_tail, 0)

    def regroup(group, final):
        def block(inner, c):
            value = wide[pl.ds(group * 32 + 2 * inner + c, JP, stride=PITCH), :]
            return jnp.concatenate([value, jnp.zeros((L - JP, L), F32)], axis=0)

        for pair in range(8):
            inners = (2 * pair, 2 * pair + 1)
            if pair in (0, 2, 4, 5, 7):
                both = [
                    jnp.concatenate([block(n, 0), block(n, 1)], axis=0).astype(BF) for n in inners
                ]
                result = dot_nt(eye_wide[...], jnp.concatenate(both, axis=1))
                turned = [
                    [result[n * L : (n + 1) * L, c * L : (c + 1) * L] for c in range(2)]
                    for n in range(2)
                ]
            else:
                turned = [[block(n, c).T for c in range(2)] for n in inners]
            for n, inner in enumerate(inners):
                for c in range(2):
                    staged[c, inner // 8, pl.ds(inner % 8, E_DEV, stride=8), :] = turned[n][c]

        if not final:
            widen(group + 1)
        for later in range(2):
            place = lax.rem(group + later, JP // 16) if not final else (1 - later) * group
            at = pl.ds(pl.multiple_of(place * 16, 16), 16)
            for e in range(later * half, (later + 1) * half):
                spot = pl.ds(e * 8, 8)
                for c in range(2):
                    tile = jnp.concatenate([staged[c, 0, spot, :], staged[c, 1, spot, :]], axis=0)
                    weights[e, at, c * L : (c + 1) * L] = tile.astype(BF)

    def regroup_step(group, carry):
        pl.when(group < 5)(lambda: load_rows(group + 1).wait())
        pl.when(group == 5)(add_tails)
        regroup(group, False)
        return carry

    load_rows(0).wait()
    widen(0)
    lax.fori_loop(0, JP // 16 - 1, regroup_step, 0)
    regroup(JP // 16 - 1, True)

    neighbours_there = jnp.int32(1)
    for shift in SHIFTS:
        there = (sub + shift >= 0) & (sub + shift < n_sub)
        neighbours_there = neighbours_there + there.astype(I32)
    pl.semaphore_wait(barrier, neighbours_there)

    def field_copy(slot):
        return pltpu.make_async_remote_copy(
            src_ref=field.at[slot],
            dst_ref=far_field.at[slot],
            send_sem=field_send.at[slot],
            recv_sem=field_recv.at[slot],
            device_id=(sub, 1 - blk),
            device_id_type=pl.DeviceIdType.MESH,
        )

    def robin_copy(slot, which):
        return pltpu.make_async_remote_copy(
            src_ref=outgoing.at[slot],
            dst_ref=arriving.at[slot, which],
            send_sem=robin_send.at[slot, which],
            recv_sem=robin_recv.at[slot, which],
            device_id=(sub + SHIFTS[which], blk),
            device_id_type=pl.DeviceIdType.MESH,
        )

    def prepare(step):
        slot = lax.rem(step, 2)
        r = lax.rem(step, ROUNDS)
        own = field[slot]
        spread = dot(own, to_trace[...]).astype(BF)
        stacked = jnp.concatenate([spread[:, f * L : (f + 1) * L] for f in range(4)], axis=0)
        traced = dot(pick[r], stacked)
        turned = jnp.where(
            (lanes // 32) % 2 == 0, pltpu.roll(traced, L - 32, 1), pltpu.roll(traced, 32, 1)
        )
        former = interface[r]
        sent = robin_re[r] * traced + robin_im[r] * turned - former.astype(F32)
        outgoing[slot] = sent.astype(BF)

    def send_all(slot):
        for which, shift in enumerate(SHIFTS):

            @pl.when((sub + shift >= 0) & (sub + shift < n_sub))
            def _(which=which):
                robin_copy(slot, which).start()

        field_copy(slot).start()

    def exchange(step):
        slot = lax.rem(step, 2)
        r = lax.rem(step, ROUNDS)
        own = field[slot]
        former = interface[r]
        pl.when(step == 1)(rest_of_constants)
        pl.when(step > 1)(lambda: sent_all(1 - slot))

        field_copy(slot).wait_recv()
        both = jnp.concatenate([own, far_field[slot]], axis=0)
        total = [base[:, p * L : (p + 1) * L] for p in range(4)]
        for f in range(4):
            gathered = dot(near[pl.ds(f * L, L), :], both).astype(BF)
            flux = [dot(gathered[:, p * L : (p + 1) * L], face_t[f]) for p in range(4)]
            re, im = couple[f, 0], couple[f, 1]
            for s in range(2):
                total[2 * s] += re * flux[2 * s] - im * flux[2 * s + 1]
                total[2 * s + 1] += re * flux[2 * s + 1] + im * flux[2 * s]
        for p in range(4):
            at = pl.ds(p * L, L)
            others = [lifted[lax.rem(r + n, ROUNDS), :, at] for n in range(1, ROUNDS)]
            rhs[:, at] = total[p] + (others[0] + others[1] + others[2])

        for which, shift in enumerate(SHIFTS):

            @pl.when((sub - shift >= 0) & (sub - shift < n_sub))
            def _(which=which):
                robin_copy(slot, which).wait_recv()

        offset = jnp.broadcast_to(matching[0, r] - sub, square)
        arrived = jnp.zeros(square, BF).astype(F32)
        for which, shift in enumerate(SHIFTS):
            arrived = jnp.where(offset == -shift, arriving[slot, which].astype(F32), arrived)
        live = rows < counts[0, r]
        updated = jnp.where(live, arrived, former.astype(F32)).astype(BF)
        interface[r] = updated
        landed = dot(lift_hot[r], updated).astype(BF)
        side = jnp.concatenate([landed[f * L : (f + 1) * L] for f in range(4)], axis=1)
        added = dot(side, from_trace[...])
        lifted[r] = added
        lay_out(rhs[...] + added)

    def sent_all(slot):
        field_copy(slot).wait_send()
        for which, shift in enumerate(SHIFTS):

            @pl.when((sub + shift >= 0) & (sub + shift < n_sub))
            def _(which=which):
                robin_copy(slot, which).wait_send()

    def lay_out(value):
        later = iota((half, L), 1) >= JP
        for c in range(2):
            for s in range(2):
                p = 2 * s + c
                first = value[0:half, p * L : (p + 1) * L]
                second = value[half:E_DEV, p * L : (p + 1) * L]
                left[0, pl.ds(c * 2 + s, half, stride=8), :] = jnp.where(later, 0.0, first)
                left[0, pl.ds(4 + c * 2 + s, half, stride=8), :] = jnp.where(later, second, 0.0)
                left[1, pl.ds(4 + c * 2 + s, half, stride=8), :] = second

    def advance(step, carry, ends=False):
        pl.when(step > 0)(lambda: exchange(step))
        following = lax.rem(step + 1, 2)
        for part in range(4):
            size = half // 4
            for pair in range(part * size, (part + 1) * size):
                spot = pl.ds(pair * 8, 8)
                vector = jnp.concatenate([left[0, spot, :], left[1, spot, 0:96]], axis=1).astype(BF)
                matrix = jnp.concatenate([weights[pair], weights[half + pair]], axis=0)
                result = dot(vector, matrix)
                product[0, spot, :] = result[:, 0:L]
                product[1, spot, :] = result[:, L : 2 * L]
            for el in range(2):
                at = pl.ds(el * half + part * size, size)
                for s in range(2):
                    first = part * size * 8 + el * 4 + s
                    pick_re = pl.ds(first, size, stride=8)
                    pick_im = pl.ds(first + 2, size, stride=8)
                    re = product[0, pick_re, :] - product[1, pick_im, :]
                    im = product[1, pick_re, :] + product[0, pick_im, :]
                    field[following, at, 2 * s * L : (2 * s + 1) * L] = re.astype(BF)
                    field[following, at, (2 * s + 1) * L : (2 * s + 2) * L] = im.astype(BF)

        if not ends:
            prepare(step + 1)
            send_all(following)

        return carry

    lay_out(base[...])
    lax.fori_loop(0, STEPS - 1, advance, 0)
    advance(jnp.int32(STEPS - 1), 0, ends=True)
    sent_all((STEPS - 1) % 2)
    final = STEPS % 2
    for s in range(2):
        for c in range(2):
            p = 2 * s + c
            turned = dot_nt(identity, field[final, :, p * L : (p + 1) * L])
            out[2 * c + s] = turned[0:DOF].astype(BF)


def shards(
    n_sub,
    source_terms,
    inverse_blocks,
    face_matrices,
    trace_matrices,
    neighbours,
    coupling,
    slot_faces,
    robin_params,
    matching,
    counts,
):
    square = (L, L)
    result = pl.pallas_call(
        functools.partial(kernel, n_sub),
        out_shape=jax.ShapeDtypeStruct((4, DOF, E_DEV), BF),
        in_specs=[pl.BlockSpec(memory_space=pl.ANY)] * 10,
        out_specs=pl.BlockSpec(memory_space=pltpu.VMEM),
        scratch_shapes=[
            pltpu.VMEM((DOF, 224, L), BF),
            pltpu.VMEM((DOF, 2, L), BF),
            pltpu.VMEM((2, 208, L), BF),
            pltpu.VMEM((2, 2, L), BF),
            pltpu.VMEM((512, L), F32),
            pltpu.VMEM((432, DOF), BF),
            pltpu.VMEM((4, DOF), BF),
            pltpu.VMEM((L, DOF), BF),
            pltpu.VMEM((2, 4, DOF), BF),
            pltpu.VMEM((4, L, L), BF),
            pltpu.VMEM((4, L), I32),
            pltpu.VMEM((4, 2, L), BF),
            pltpu.VMEM((4, L), I32),
            pltpu.VMEM((2, 4, L), BF),
            pltpu.SMEM((1, 4), I32),
            pltpu.SMEM((1, 4), I32),
            pltpu.VMEM((JP * PITCH + 8, L), F32),
            pltpu.VMEM((2, 2, 8 * E_DEV, L), F32),
            pltpu.VMEM((E_DEV, JP, 2 * L), BF),
            pltpu.VMEM(square, BF),
            pltpu.VMEM((4 * L, 2 * L), BF),
            pltpu.VMEM((ROUNDS, L, 4 * L), BF),
            pltpu.VMEM((ROUNDS, 4 * L, L), BF),
            pltpu.VMEM((4 * L, 4 * L), BF),
            pltpu.VMEM((4 * L, 4 * L), BF),
            pltpu.VMEM((ROUNDS, L, L), F32),
            pltpu.VMEM((ROUNDS, L, L), F32),
            pltpu.VMEM((4, 2, L, L), F32),
            pltpu.VMEM((E_DEV, 4 * L), F32),
            pltpu.VMEM((ROUNDS, E_DEV, 4 * L), F32),
            pltpu.VMEM((ROUNDS, L, L), BF),
            pltpu.VMEM((E_DEV, 4 * L), F32),
            pltpu.VMEM((2, 4 * E_DEV, L), F32),
            pltpu.VMEM((2, 4 * E_DEV, L), F32),
            pltpu.VMEM((2, E_DEV, 4 * L), BF),
            pltpu.VMEM((2, E_DEV, 4 * L), BF),
            pltpu.VMEM((2, L, L), BF),
            pltpu.VMEM((2, 4, L, L), BF),
            pltpu.VMEM(square, BF),
            pltpu.VMEM((2 * L, 2 * L), BF),
            pltpu.SemaphoreType.DMA((14,)),
            pltpu.SemaphoreType.DMA((6,)),
            pltpu.SemaphoreType.DMA((2,)),
            pltpu.SemaphoreType.DMA((2,)),
            pltpu.SemaphoreType.DMA((2, 4)),
            pltpu.SemaphoreType.DMA((2, 4)),
        ],
        compiler_params=pltpu.CompilerParams(
            collective_id=0, has_side_effects=True, vmem_limit_bytes=56 * 2**20
        ),
    )(
        jnp.transpose(inverse_blocks, (1, 2, 0, 3)),
        source_terms,
        jnp.transpose(face_matrices, (1, 0, 2)),
        jnp.transpose(trace_matrices, (1, 0, 2)),
        jnp.transpose(neighbours),
        jnp.transpose(coupling, (1, 2, 0)),
        slot_faces[0],
        robin_params[:, 0],
        jnp.transpose(matching),
        jnp.transpose(counts[:, :, 0]),
    )
    return result.reshape(2, 2, DOF, E_DEV).transpose(0, 2, 1, 3)


def solution(mesh):
    in_specs = (
        P(None, None, None, ("sub", "blk")),
        P(None, None, None, ("sub", "blk")),
        P(),
        P(),
        P(("sub", "blk"), None),
        P(("sub", "blk"), None, None),
        P("sub", None, "blk"),
        P(None, "sub", None, "blk"),
        P(None, "sub"),
        P(None, "sub", "blk"),
    )
    out_specs = P(None, None, None, ("sub", "blk"))
    body = functools.partial(shards, mesh.shape["sub"])
    return jax.shard_map(body, mesh=mesh, in_specs=in_specs, out_specs=out_specs, check_vma=False)
```
